128 devices in a mesh: dp: 16 (over x, z), vocab: 8 (over y, core).
Axes of the slice: x: 4, y: 4, z: 4, core: 2. Of those that a mesh axis runs over, the one named last changes fastest.
Arguments:
- hidden: bfloat16 [1024, 4096], P('dp', 'vocab'), may hold values from -400 to 400
- output_head_matrix: bfloat16 [4096, 151936], P(None, ('dp', 'vocab')), may hold values from -0.09375 to 0.09375
- row_counts: int32 [16], replicated, may hold values from 1 to 64, 512 in all
- token_ids: int32 [512], P('dp'), may hold values from 0 to 151935
- segment_ids: int32 [512], P('dp'), may hold values from 0 to 31, never falling along the last dimension, each value on 1 to 64 neighbouring positions
- cotangent: float32 [512], P('dp'), may hold values from -6 to 6
Outputs:
- logprobs: float32 [512], P('dp')
- grad_hidden: bfloat16 [1024, 4096], P('dp', 'vocab')
The draws below stay inside these ranges and needn't reach their ends.
Inputs may be any that keep to these rules, and one draw needn't show every extreme that they name: `row_counts`: live rows of each index of dp; they sum to 512, one index holds 64. `segment_ids`: never falling; each segment has 1 to 64 positions, one exactly 64.
All inputs are finite; a program needn't handle non-finite values.
Results may differ from the reference program's by a relative error of at most 0.0034.
Values may be sent and summed in bfloat16 or wider, within the bound.
No kernel may reach another device: no remote copies, remote signals or barrier semaphores. Data moves between devices by JAX's collectives and lax.ppermute only.
A program may use at most 128 MiB of HBM per device.

```python
import math
import jax
import jax.numpy as jnp
import numpy as np
from jax import lax

D = 4096
V = 151936
TOK_DEV = 32
CAP = 64
TOTAL = 512
ROWS_IN = 1024
SEGS = 32
SEG_MOST = 64
N_DP = 16
DEVICES = 128


def draw_hidden(key, part):
    key = jax.random.fold_in(key, 7)
    first_key = jax.random.fold_in(key, 0)
    values = jnp.clip(jax.random.normal(first_key, (ROWS_IN, D), jnp.float32), -4.0, 4.0)
    return values.astype(jnp.bfloat16)


def plant(values, key, smallest, high):
    place = [jax.random.randint(jax.random.fold_in(key, axis), (), 0, length) for axis, length in enumerate(values.shape)]
    widest = values.shape.index(max(values.shape))
    neighbour = place[:widest] + [(place[widest] + 1) % values.shape[widest]] + place[widest + 1:]
    return values.at[tuple(place)].set(smallest).at[tuple(neighbour)].set(high)


def block_levels(key, extent, cuts, low, largest):
    factor_of = 1.0
    for axis_at, blocks in cuts:
        draws = jax.random.uniform(jax.random.fold_in(jax.random.fold_in(key, 6), axis_at), (blocks,), jnp.float32, low / len(cuts), largest / len(cuts))
        factor_of = factor_of * jnp.repeat(jnp.exp(draws), extent[axis_at] // blocks).reshape((-1,) + (1,) * (len(extent) - 1 - axis_at))
    return factor_of


def skewed_wide(stream_key, dims, count, skew):
    loads = [min(1 << octave, count + 1 - (1 << octave)) * (1 << 20) // math.isqrt((1 << octave) ** skew) + 1 for octave in range((count + 1).bit_length()) if 1 << octave <= count]
    deviation = 1 + sum(loads) // (1 << 30)
    listing = np.cumsum(np.array([max(1, weight // deviation) for weight in loads]))
    pick = jax.random.randint(jax.random.fold_in(stream_key, 1), dims, 0, int(listing[len(loads) - 1]))
    start = jnp.left_shift(1, jnp.searchsorted(jnp.asarray(listing, jnp.int32), pick, side="right").astype(jnp.int32))
    grade = start - 1 + jax.random.randint(jax.random.fold_in(stream_key, 4), dims, 0, 1 << 30) % jnp.minimum(start, count + 1 - start)
    return jax.random.permutation(jax.random.fold_in(stream_key, 2), count)[grade].astype(jnp.int32)


def split_up(amount, total, limit, skew):
    loads = [(1 << 20) // math.isqrt(standing ** skew) + 1 for standing in range(2, amount + 1)]
    surplus, given = total - limit - (amount - 1), [1] * (amount - 1)
    while surplus > 0:
        free = [i for i in range(amount - 1) if given[i] < limit]
        whole, budget = sum([loads[i] for i in free]), surplus
        for i in free:
            extra = min(limit - given[i], max(1, budget * loads[i] // whole), surplus)
            given[i] = given[i] + extra
            surplus = surplus - extra
    return np.array([limit] + given)


def ragged_sizes(own_key, amount, total, limit, lean):
    if amount == 2:
        one = jax.random.randint(own_key, (), max(1, total - limit), min(limit, total - 1) + 1)
        return jnp.stack([one, total - one])
    tallies = jnp.asarray(split_up(amount, total, limit, lean), jnp.int32)
    couples = (amount - 1) // 2
    source_of, sink = tallies[1:1 + 2 * couples:2], tallies[2:2 + 2 * couples:2]
    margin = jnp.minimum(source_of - 1, limit - sink)
    moved = jax.random.randint(jax.random.fold_in(own_key, 1), (couples,), 0, 1 << 20) % (margin + 1)
    tallies = tallies.at[1:1 + 2 * couples:2].set(source_of - moved).at[2:2 + 2 * couples:2].set(sink + moved)
    return tallies[jax.random.permutation(jax.random.fold_in(own_key, 2), amount)]


def gaussian(own_key, extent, spread, limit, shards=(), kind=jnp.bfloat16):
    entries = spread * jax.random.normal(own_key, extent, jnp.float32)
    if shards:
        entries = entries * block_levels(own_key, extent, shards, -0.22, 0.18)
    return jnp.clip(entries, -limit, limit).astype(kind)


def setup_inputs(seed: int = 0) -> dict:
    keys = jax.random.split(jax.random.key(seed), 7)
    hidden = draw_hidden(jax.random.fold_in(keys[6], 71), 0)
    output_head_matrix = gaussian(keys[1], (D, V), D ** -0.5, 0.09375, ((1, 128),))
    row_counts = ragged_sizes(keys[2], N_DP, TOK_DEV * N_DP, CAP, 2).astype(jnp.int32)
    token_ids = plant(skewed_wide(keys[3], (TOTAL,), V, 2), jax.random.fold_in(keys[3], 3), 0, V - 1).astype(jnp.int32)
    segment_ids = jnp.searchsorted(jnp.cumsum(ragged_sizes(keys[4], SEGS, TOTAL, SEG_MOST, 2)), jnp.arange(TOTAL), side="right").astype(jnp.int32)
    cotangent = gaussian(keys[5], (TOTAL,), 1.0, 6.0, ((0, 16),), jnp.float32)
    return dict(hidden=hidden, output_head_matrix=output_head_matrix, row_counts=row_counts, token_ids=token_ids, segment_ids=segment_ids, cotangent=cotangent)


freq_weight = 0.4
presence_weight = 0.8


def reference(hidden, output_head_matrix, row_counts, token_ids, segment_ids, cotangent):
    ends = jnp.cumsum(row_counts).astype(jnp.int32)
    starts = (ends - row_counts).astype(jnp.int32)
    index = jnp.arange(TOTAL, dtype=jnp.int32)
    rollout = (index % TOK_DEV) * N_DP + index // TOK_DEV
    source = jnp.sum((rollout[:, None] >= ends[None, :]).astype(jnp.int32), axis=1).astype(jnp.int32)
    source_row = (source * CAP + rollout - starts[source]).astype(jnp.int32)
    packed = hidden[source_row]
    prior_token_hits = ((segment_ids[:, None] == segment_ids[None, :]) & (index[None, :] < index[:, None])).astype(jnp.bfloat16)
    block_cols = V // DEVICES

    def forward_block(block):
        first_col = (block * block_cols).astype(jnp.int32)
        weight_cols = lax.dynamic_slice_in_dim(output_head_matrix, first_col, block_cols, 1)
        logits = jnp.dot(packed, weight_cols, preferred_element_type=jnp.float32)
        hits = token_ids[:, None] == first_col + jnp.arange(block_cols, dtype=jnp.int32)[None, :]
        counts = jnp.dot(prior_token_hits, hits.astype(jnp.bfloat16), preferred_element_type=jnp.float32)
        scores = logits - freq_weight * counts - presence_weight * (counts > 0).astype(jnp.float32)
        return scores, jnp.sum(jnp.where(hits, scores, jnp.zeros_like(scores)), axis=1)

    blocks = jnp.arange(DEVICES, dtype=jnp.int32)
    scores, picked = lax.map(forward_block, blocks)
    top = jnp.max(scores, axis=(0, 2))
    total = jnp.sum(jnp.exp(scores - top[None, :, None]), axis=(0, 2))
    logprobs = jnp.sum(picked, axis=0) - top - jnp.log(total)

    def backward_block(summed, inputs):
        block_logit_values, block = inputs
        first_col = (block * block_cols).astype(jnp.int32)
        weight_cols = lax.dynamic_slice_in_dim(output_head_matrix, first_col, block_cols, 1)
        hits = token_ids[:, None] == first_col + jnp.arange(block_cols, dtype=jnp.int32)[None, :]
        residual = (hits.astype(jnp.float32) - jnp.exp(block_logit_values - top[:, None]) / total[:, None]).astype(jnp.bfloat16)
        return summed + jnp.dot(residual, weight_cols.T, preferred_element_type=jnp.float32), None

    summed, _ = lax.scan(backward_block, jnp.zeros((TOTAL, D), jnp.float32), (scores, blocks))
    scaled = (summed * cotangent[:, None]).astype(jnp.bfloat16)
    grad_hidden = jnp.zeros((ROWS_IN, D), jnp.bfloat16).at[source_row].set(scaled)
    return logprobs, grad_hidden
```

```python
import functools

import jax
import jax.numpy as jnp
from jax import lax
from jax.experimental import pallas as pl
from jax.experimental.pallas import tpu as pltpu
from jax.sharding import PartitionSpec as P

freq_weight = 0.4
presence_weight = 0.8

N_DP, N_VOC = 16, 8
FEAT = 512
BF, F32, I32 = jnp.bfloat16, jnp.float32, jnp.int32
MIB = 1 << 20


def params(limit=32):
    return pltpu.CompilerParams(vmem_limit_bytes=limit * MIB)


def coords():
    dp, voc = lax.axis_index("dp"), lax.axis_index("vocab")
    return dp // 4, lax.rem(dp, 4), voc // 2, lax.rem(voc, 2)


def flat(x, z, y, c):
    return x * 32 + z * 8 + y * 2 + c


def shift_perm(axes, k):
    pairs = []
    for x in range(4):
        for z in range(4):
            for y in range(4):
                for c in range(2):
                    to = dict(x=x, z=z, y=y, c=c)
                    to[axes[c]] = (to[axes[c]] + k) % 4
                    pairs.append((flat(x, z, y, c), flat(**to)))
    return pairs


CORE_PERM = [(i, i ^ 1) for i in range(N_DP * N_VOC)]


def permute(v, pairs):
    return lax.ppermute(v, ("dp", "vocab"), pairs)


def iota(shape, dim):
    return lax.broadcasted_iota(I32, shape, dim)


VM = pl.BlockSpec(memory_space=pltpu.VMEM)
SM = pl.BlockSpec(memory_space=pltpu.SMEM)
ANY = pl.BlockSpec(memory_space=pl.ANY)


def my_start(rc_ref, dp):
    start = jnp.int32(0)
    for s in range(N_DP):
        start = start + jnp.where(s < dp, rc_ref[s], 0)
    return start


def pack_kernel(rc_ref, hid_ref, tok_ref, seg_ref, out_ref):
    dp = lax.axis_index("dp")
    start, count = my_start(rc_ref, dp), rc_ref[dp]
    row, col = iota((128, 64), 0), iota((128, 64), 1)
    t = row & 7
    src = t * N_DP + (((row >> 3) - start) & 15)
    sel = (t < 4) & (col == src) & (col < count)
    out_ref[...] = jnp.dot(sel.astype(F32).astype(BF), hid_ref[...], preferred_element_type=F32).astype(BF)
    t32 = iota((128, 32), 0) & 7
    tok, seg = tok_ref[...], seg_ref[...]
    digit = jnp.where(t32 == 4, tok & 255, jnp.where(t32 == 5, (tok >> 8) & 255, jnp.where(t32 == 6, tok >> 16, seg)))
    old = out_ref[:, 0:32].astype(F32)
    out_ref[:, 0:32] = jnp.where(t32 >= 4, digit.astype(F32), old).astype(BF)


def placing(rc_ref, shape, slot_dim):
    dp = lax.axis_index("dp")
    k, pos = iota(shape, slot_dim), iota(shape, 1 - slot_dim)
    s, t = k >> 3, k & 7
    start = jnp.zeros(shape, I32)
    count = jnp.zeros(shape, I32)
    run = jnp.int32(0)
    for i in range(N_DP):
        start = jnp.where(s == i, run, start)
        count = jnp.where(s == i, rc_ref[i], count)
        run = run + rc_ref[i]
    offset = (dp - start) & 15
    base = (start + offset - dp) >> 4
    sel = (t < 4) & (t * N_DP + offset < count) & (base + t == pos)
    return sel.astype(F32).astype(BF)


def unpack_kernel(rc_ref, arr_ref, out_ref):
    sel = placing(rc_ref, (32, 128), 1)
    out_ref[...] = jnp.dot(sel, arr_ref[...], preferred_element_type=F32).astype(BF)


def place_kernel(mode, a0, a1, a2, a3, out_ref):
    x, z, y, c = coords()
    own = z if mode == "z" else jnp.where(c == 0, x, y)
    for d, a in enumerate((a0, a1, a2, a3)):
        out_ref[pl.ds((own + d) & 3, 1)] = a[...][None]


def column(row):
    wide = jnp.broadcast_to(row, (128, row.shape[1]))
    return jnp.transpose(wide)[:, 0:1]


def code_kernel(cols, tok_ref, seg_ref, out_ref):
    dp, voc = lax.axis_index("dp"), lax.axis_index("vocab")
    tok, seg = tok_ref[...], seg_ref[...]
    tok_col = column(tok.astype(F32)).astype(I32)
    seg_col = column(seg.astype(F32)).astype(I32)
    prior = (seg_col == seg) & (iota((512, 512), 1) < iota((512, 512), 0))
    prior = prior.astype(F32).astype(BF)
    first = (dp * N_VOC + voc) * cols
    hits = (tok_col == first + iota((512, cols), 1)).astype(F32)
    counts = jnp.dot(prior, hits.astype(BF), preferred_element_type=F32)
    out_ref[...] = (counts + 128.0 * hits).astype(BF)


def scores_kernel(cols, *refs):
    blocks, (w_ref, code_ref, s_ref, stat_ref, xs, ws, ss, xsem, wsem) = refs[:8], refs[8:]
    x, z, y, c = coords()
    for k in range(4):
        pltpu.make_async_copy(w_ref.at[pl.ds(k * 1024, 1024)], ws.at[k], wsem.at[k]).start()
    copies = []
    for n in range(8):
        core = c if n < 4 else 1 - c
        own = jnp.where(core == 0, y, x)
        p = (own + n % 4) & 3
        for q in range(4):
            xx = jnp.where(core == 0, q, p)
            yy = jnp.where(core == 0, p, q)
            dst = xs.at[pl.ds(pl.multiple_of(xx * 128, 128), 128), pl.ds(pl.multiple_of((yy * 2 + core) * FEAT, FEAT), FEAT)]
            copies.append(pltpu.make_async_copy(blocks[n].at[q], dst, xsem.at[n * 4 + q]))
    for cp in copies:
        cp.start()
    for cp in copies:
        cp.wait()
    for k in range(4):
        pltpu.make_async_copy(w_ref.at[pl.ds(k * 1024, 1024)], ws.at[k], wsem.at[k]).wait()
        part = jnp.dot(xs[:, k * 1024:(k + 1) * 1024], ws[k], preferred_element_type=F32)
        if k == 0:
            s_ref[...] = part
        else:
            s_ref[...] += part

    def rows(i, _):
        at = pl.ds(pl.multiple_of(i * 32, 32), 32)
        code = code_ref[at, :].astype(F32)
        hit = code > 127.5
        counts = jnp.where(hit, code - 128.0, code)
        s = s_ref[at, :] - freq_weight * counts - presence_weight * (counts > 0).astype(F32)
        s_ref[at, :] = s
        m = jnp.max(s, axis=1, keepdims=True)
        ss[at, 0:1] = m
        ss[at, 1:2] = jnp.sum(jnp.exp(s - m), axis=1, keepdims=True)
        ss[at, 2:3] = jnp.sum(jnp.where(hit, s, 0.0), axis=1, keepdims=True)
        return _

    lax.fori_loop(0, 16, rows, 0)
    flat_stats = jnp.transpose(ss[...])
    for j in range(3):
        for k in range(4):
            piece = flat_stats[j:j + 1, k * 128:(k + 1) * 128]
            for n in range(N_VOC):
                stat_ref[n, j * 4 + k:j * 4 + k + 1, :] = piece
    for n in range(N_VOC):
        stat_ref[n, 12:16, :] = jnp.zeros((4, 128), F32)


def merge(st_ref, n):
    m = st_ref[0, 0:4, :]
    for i in range(1, n):
        m = jnp.maximum(m, st_ref[i, 0:4, :])
    total = jnp.zeros_like(m)
    picked = jnp.zeros_like(m)
    for i in range(n):
        total = total + st_ref[i, 4:8, :] * jnp.exp(st_ref[i, 0:4, :] - m)
        picked = picked + st_ref[i, 8:12, :]
    return m, total, picked


def merge_kernel(st_ref, out_ref):
    m, total, picked = merge(st_ref, N_VOC)
    for n in range(N_DP):
        out_ref[n, 0:4, :] = m
        out_ref[n, 4:8, :] = total
        out_ref[n, 8:12, :] = picked
        out_ref[n, 12:16, :] = jnp.zeros((4, 128), F32)


def grad_kernel(cols, w_ref, s_ref, code_ref, st_ref, keep_ref, send_ref, lp_ref, ws, rs, cs, lps, wsem):
    x, z, y, c = coords()

    def head(i):
        block = (i & 3) * 2 + jnp.where(i < 4, 1 - c, c)
        return pltpu.make_async_copy(w_ref.at[pl.ds(pl.multiple_of(block * FEAT, FEAT), FEAT)], ws.at[i], wsem.at[i])

    for i in range(8):
        head(i).start()
    m, total, picked = merge(st_ref, N_DP)
    lps[0:4, :] = picked - m - jnp.log(total)
    mine = lps[pl.ds(x, 1), :]
    mine = pltpu.roll(mine, (128 - 32 * z) & 127, 1)
    lp_ref[...] = mine[:, 0:32]
    for k in range(4):
        cs[k * 128:(k + 1) * 128, 0:128] = jnp.transpose(jnp.broadcast_to(m[k:k + 1, :], (128, 128)))
        cs[k * 128:(k + 1) * 128, 128:256] = jnp.transpose(jnp.broadcast_to(total[k:k + 1, :], (128, 128)))

    def rows(i, _):
        at = pl.ds(pl.multiple_of(i * 32, 32), 32)
        hit = (code_ref[at, :].astype(F32) > 127.5).astype(F32)
        p = jnp.exp(s_ref[at, :] - cs[at, 0:1]) / cs[at, 128:129]
        rs[at, :] = (hit - p).astype(BF)
        return _

    lax.fori_loop(0, 16, rows, 0)

    def product(i):
        return lax.dot_general(rs[...], ws[i], (((1,), (1,)), ((), ())), preferred_element_type=F32)

    for half, core, out_ref in ((0, 1 - c, send_ref), (4, c, keep_ref)):
        for yy in range(4):
            head(half + yy).wait()
            v = product(half + yy)
            for xx in range(4):
                p = jnp.where(core == 0, yy, xx)
                q = jnp.where(core == 0, xx, yy)
                out_ref[p, q] = v[xx * 128:(xx + 1) * 128].astype(out_ref.dtype)


def core_sum_kernel(keep_ref, got_ref, own_ref, b1, b2, b3):
    x, z, y, c = coords()
    own = jnp.where(c == 0, y, x)
    for d, out in enumerate((own_ref, b1, b2, b3)):
        p = (own + d) & 3
        for q in range(4):
            out[q] = (keep_ref[p, q] + got_ref[p, q].astype(F32)).astype(out.dtype)


def ring_sum_kernel(mode, own_in, r1, r2, r3, own_ref, b1, b2, b3):
    x, z, y, c = coords()
    own = z if mode == "z" else jnp.where(c == 0, x, y)
    for d, out in enumerate((own_ref, b1, b2, b3)):
        q = (own + d) & 3
        v = own_in[q].astype(F32) + r1[q].astype(F32) + r2[q].astype(F32) + r3[q].astype(F32)
        out[...] = v.astype(out.dtype)


def return_kernel(rc_ref, cot_ref, own_in, r1, r2, r3, out_ref):
    v = own_in[...] + r1[...] + r2[...] + r3[...]
    scaled = (v * cot_ref[...]).astype(BF)
    sel = placing(rc_ref, (128, 32), 0)
    out_ref[...] = jnp.dot(sel, scaled, preferred_element_type=F32).astype(BF)


def slots_kernel(rc_ref, arr_ref, out_ref):
    dp = lax.axis_index("dp")
    start, count = my_start(rc_ref, dp), rc_ref[dp]
    j, k = iota((64, 128), 0), iota((64, 128), 1)
    at = ((start + j) & 15) * 8 + (j >> 4)
    sel = ((k == at) & (j < count)).astype(F32).astype(BF)
    out_ref[...] = jnp.dot(sel, arr_ref[...], preferred_element_type=F32).astype(BF)


def sds(shape, dtype):
    return jax.ShapeDtypeStruct(shape, dtype)


def call(kernel, ins, outs, in_specs=None, scratch=(), limit=32, cost=None):
    multi = isinstance(outs, (list, tuple))
    return pl.pallas_call(
        kernel,
        out_shape=outs,
        in_specs=in_specs or [VM] * len(ins),
        out_specs=[VM] * len(outs) if multi else VM,
        scratch_shapes=list(scratch),
        compiler_params=params(limit),
        cost_estimate=cost,
    )(*ins)


def cost(flops, nbytes):
    return pl.CostEstimate(flops=flops, bytes_accessed=nbytes, transcendentals=0)


def per_device(hidden, head, row_counts, token_ids, segment_ids, cotangent):
    cols = head.shape[1]
    outgoing = call(
        pack_kernel,
        (row_counts, hidden, token_ids.reshape(1, 32), segment_ids.reshape(1, 32)),
        sds((128, FEAT), BF),
        in_specs=[SM, VM, VM, VM],
    )
    arrived = lax.all_to_all(outgoing.reshape(N_DP, 8, FEAT), "dp", 0, 0, tiled=True)
    flat_arrived = arrived.reshape(128, FEAT)
    packed = call(unpack_kernel, (row_counts, flat_arrived), sds((32, FEAT), BF), in_specs=[SM, VM])
    digits = arrived[:, 4:8, 0:32].astype(F32)
    tokens = (digits[:, 0] + 256.0 * digits[:, 1] + 65536.0 * digits[:, 2]).astype(I32).reshape(1, 512)
    segments = digits[:, 3].astype(I32).reshape(1, 512)

    first = [packed] + [permute(packed, shift_perm("zz", 4 - d)) for d in (1, 2, 3)]
    g1 = call(functools.partial(place_kernel, "z"), first, sds((4, 32, FEAT), BF)).reshape(128, FEAT)
    second = [g1] + [permute(g1, shift_perm("xy", 4 - d)) for d in (1, 2, 3)]
    g2 = call(functools.partial(place_kernel, "xy"), second, sds((4, 128, FEAT), BF))
    third = [g2] + [permute(g2, shift_perm("yx", 4 - d)) for d in (1, 2, 3)]
    other = [permute(v, CORE_PERM) for v in third]
    code = call(
        functools.partial(code_kernel, cols), (tokens, segments), sds((512, cols), BF), cost=cost(2 * 512 * 512 * 1280, 3 * MIB)
    )

    s, stats = call(
        functools.partial(scores_kernel, cols),
        (*third, *other, head, code),
        [sds((512, cols), F32), sds((N_VOC, 16, 128), F32)],
        in_specs=[ANY] * 9 + [VM],
        scratch=[
            pltpu.VMEM((512, 4096), BF),
            pltpu.VMEM((4, 1024, cols), BF),
            pltpu.VMEM((512, 128), F32),
            pltpu.SemaphoreType.DMA((32,)),
            pltpu.SemaphoreType.DMA((4,)),
        ],
        limit=40,
        cost=cost(2 * 512 * 4096 * 1280, 16 * MIB),
    )
    stats = lax.all_to_all(stats, "vocab", 0, 0, tiled=True)
    stats = call(merge_kernel, (stats,), sds((N_DP, 16, 128), F32))
    stats = lax.all_to_all(stats, "dp", 0, 0, tiled=True)

    keep, send, logprobs = call(
        functools.partial(grad_kernel, cols),
        (head, s, code, stats),
        [sds((4, 4, 128, FEAT), F32), sds((4, 4, 128, FEAT), BF), sds((1, 32), F32)],
        in_specs=[ANY, VM, VM, VM],
        scratch=[
            pltpu.VMEM((8, FEAT, cols), BF),
            pltpu.VMEM((512, cols), BF),
            pltpu.VMEM((512, 256), F32),
            pltpu.VMEM((8, 128), F32),
            pltpu.SemaphoreType.DMA((8,)),
        ],
        limit=48,
        cost=cost(2 * 512 * 4096 * 1280, 16 * MIB),
    )
    got = permute(send, CORE_PERM)
    own, *out = call(
        core_sum_kernel, (keep, got), [sds((4, 128, FEAT), F32)] + [sds((4, 128, FEAT), BF)] * 3
    )
    got = [permute(v, shift_perm("yx", d + 1)) for d, v in enumerate(out)]
    own, *out = call(
        functools.partial(ring_sum_kernel, "xy"), (own, *got), [sds((128, FEAT), F32)] + [sds((128, FEAT), F32)] * 3
    )
    got = [permute(v, shift_perm("xy", d + 1)) for d, v in enumerate(out)]
    own, *out = call(
        functools.partial(ring_sum_kernel, "z"),
        [v.reshape(4, 32, FEAT) for v in (own, *got)],
        [sds((32, FEAT), F32)] * 4,
    )
    got = [permute(v, shift_perm("zz", d + 1)) for d, v in enumerate(out)]
    returning = call(
        return_kernel,
        (row_counts, cotangent.reshape(32, 1), own, *got),
        sds((128, FEAT), BF),
        in_specs=[SM] + [VM] * 5,
    )
    returned = lax.all_to_all(returning.reshape(N_DP, 8, FEAT), "dp", 0, 0, tiled=True)
    grad_hidden = call(
        slots_kernel, (row_counts, returned.reshape(128, FEAT)), sds((64, FEAT), BF), in_specs=[SM, VM]
    )
    return logprobs.reshape(32), grad_hidden


def solution(mesh):
    return jax.shard_map(
        per_device,
        mesh=mesh,
        in_specs=(P("dp", "vocab"), P(None, ("dp", "vocab")), P(), P("dp"), P("dp"), P("dp")),
        out_specs=(P("dp"), P("dp", "vocab")),
        check_vma=False,
    )
```

```python
import functools

import jax
import jax.numpy as jnp
from jax import lax
from jax.experimental import pallas as pl
from jax.experimental.pallas import tpu as pltpu
from jax.sharding import PartitionSpec as P

freq_weight = 0.4
presence_weight = 0.8

N_DP, N_VOC = 16, 8
FEAT = 512
BF, F32, I32 = jnp.bfloat16, jnp.float32, jnp.int32
MIB = 1 << 20


def params(limit=32):
    return pltpu.CompilerParams(vmem_limit_bytes=limit * MIB)


def coords():
    dp, voc = lax.axis_index("dp"), lax.axis_index("vocab")
    return dp // 4, lax.rem(dp, 4), voc // 2, lax.rem(voc, 2)


def flat(x, z, y, c):
    return x * 32 + z * 8 + y * 2 + c


def shift_perm(axes, k):
    pairs = []
    for x in range(4):
        for z in range(4):
            for y in range(4):
                for c in range(2):
                    to = dict(x=x, z=z, y=y, c=c)
                    to[axes[c]] = (to[axes[c]] + k) % 4
                    pairs.append((flat(x, z, y, c), flat(**to)))
    return pairs


def pairing(axis, bits, cores=(0, 1)):
    pairs = []
    for x in range(4):
        for z in range(4):
            for y in range(4):
                for c in cores:
                    to = dict(x=x, z=z, y=y, c=c)
                    to[axis] ^= bits
                    pairs.append((flat(x, z, y, c), flat(**to)))
    return pairs


CORE_PERM = [(i, i ^ 1) for i in range(N_DP * N_VOC)]


def permute(v, pairs):
    return lax.ppermute(v, ("dp", "vocab"), pairs)


def iota(shape, dim):
    return lax.broadcasted_iota(I32, shape, dim)


VM = pl.BlockSpec(memory_space=pltpu.VMEM)
SM = pl.BlockSpec(memory_space=pltpu.SMEM)
HBM = pl.BlockSpec(memory_space=pltpu.HBM)


def my_start(rc_ref, dp):
    start = jnp.int32(0)
    for s in range(N_DP):
        start = start + jnp.where(s < dp, rc_ref[s], 0)
    return start


def pack_kernel(rc_any, hid_any, tok_any, seg_any, cot_any, out_ref, rc_ref, hid_ref, tok_ref, seg_ref, cot_ref, sems):
    pairs = ((rc_any, rc_ref), (hid_any, hid_ref), (tok_any, tok_ref), (seg_any, seg_ref), (cot_any, cot_ref))
    copies = [pltpu.make_async_copy(a, b, sems.at[i]) for i, (a, b) in enumerate(pairs)]
    for cp in copies:
        cp.start()
    for cp in copies:
        cp.wait()
    dp = lax.axis_index("dp")
    start, count = my_start(rc_ref, dp), rc_ref[dp]
    row, col = iota((64, 64), 0), iota((64, 64), 1)
    target = (row >> 4) * 4 + (row & 3)
    src = ((row >> 2) & 3) * N_DP + ((target - start) & 15)
    sel = (col == src) & (col < count)
    rows = jnp.dot(sel.astype(F32).astype(BF), hid_ref[...], preferred_element_type=F32).astype(BF)
    kind = iota((8, 32), 0)
    tok, cot = tok_ref[...], cot_ref[...]
    digit = jnp.where(kind == 0, tok & 255, jnp.where(kind == 1, (tok >> 8) & 255, jnp.where(kind == 2, tok >> 16, seg_ref[...])))
    high = cot.astype(BF).astype(F32)
    mid = (cot - high).astype(BF).astype(F32)
    low = cot - high - mid
    digit = jnp.where(kind < 4, digit.astype(F32), jnp.where(kind == 4, high, jnp.where(kind == 5, mid, low))).astype(BF)
    for a in range(N_DP):
        out_ref[a, 0:16, :] = rows[(a // 4) * 16:(a // 4) * 16 + 16]
        out_ref[a, 16:24, :] = jnp.zeros((8, FEAT), BF)
        out_ref[a, 16:24, 0:32] = digit


def placing(rc_ref, shape, slot_dim, per_source):
    x = lax.axis_index("dp") // 4
    k, row = iota(shape, slot_dim), iota(shape, 1 - slot_dim)
    s = k >> 4 if per_source == 16 else (k * 2731) >> 16
    u = k - s * per_source
    t, z = u >> 2, u & 3
    start = jnp.zeros(shape, I32)
    count = jnp.zeros(shape, I32)
    run = jnp.int32(0)
    for i in range(N_DP):
        start = jnp.where(s == i, run, start)
        count = jnp.where(s == i, rc_ref[i], count)
        run = run + rc_ref[i]
    a = x * 4 + z
    offset = (a - start) & 15
    base = (start + offset - a) >> 4
    sel = (u < 16) & (t * N_DP + offset < count) & (z * 32 + base + t == row)
    return sel.astype(F32).astype(BF)


def unpack_kernel(rc_ref, arr_ref, out_ref):
    sel = placing(rc_ref, (128, 384), 1, 24)
    out_ref[...] = jnp.dot(sel, arr_ref[...], preferred_element_type=F32).astype(BF)


def place_kernel(a0, a1, a2, a3, out_ref):
    x, z, y, c = coords()
    own = jnp.where(c == 0, x, y)
    for d, a in enumerate((a0, a1, a2, a3)):
        out_ref[pl.ds((own + d) & 3, 1)] = a[...][None]


def column(row):
    wide = jnp.broadcast_to(row, (128, row.shape[1]))
    return jnp.transpose(wide)[:, 0:1]


def code_kernel(cols, tok_ref, seg_ref, hit_ref, start_ref):
    dp, voc = lax.axis_index("dp"), lax.axis_index("vocab")
    tok, seg = tok_ref[...], seg_ref[...]
    tok_col = column(tok.astype(F32)).astype(I32)
    seg_col = column(seg.astype(F32)).astype(I32)
    prior = (seg_col == seg) & (iota((512, 512), 1) < iota((512, 512), 0))
    prior = prior.astype(F32).astype(BF)
    first = (dp * N_VOC + voc) * cols
    hits = (tok_col == first + iota((512, cols), 1)).astype(F32).astype(BF)
    hit_ref[...] = hits
    counts = jnp.dot(prior, hits, preferred_element_type=F32)
    start_ref[...] = -(freq_weight * counts) - presence_weight * (counts > 0).astype(F32)


def features(yy, core):
    return pl.ds(pl.multiple_of((yy * 2 + core) * FEAT, FEAT), FEAT)


def block_scores(ds, zero, one, head_ref, s_in, s_ref):
    x, z, y, c = coords()
    dims = (((1,), (1,)), ((), ()))
    if zero is not None:
        part = s_in[...]
        for d, block in zip(ds, zero):
            w = head_ref[:, features((y + d) & 3, 0)]
            part += lax.dot_general(block[...].reshape(512, FEAT), w, dims, preferred_element_type=F32)
        s_ref[...] = part
    else:
        s_ref[...] = s_in[...]
    if one is not None:
        part = None
        for q in range(4):
            rows = jnp.concatenate([block[q] for block in one], axis=0)
            v = lax.dot_general(rows, head_ref[:, features(q, 1)], dims, preferred_element_type=F32)
            part = v if part is None else part + v
        for i, d in enumerate(ds):
            s_ref[pl.ds(pl.multiple_of(((x + d) & 3) * 128, 128), 128), :] += part[i * 128:(i + 1) * 128]


def both_scores(ds, own, other, head_ref, s_in, s_ref):
    c = coords()[3]

    @pl.when(c == 0)
    def _():
        block_scores(ds, own, other, head_ref, s_in, s_ref)

    @pl.when(c == 1)
    def _():
        block_scores(ds, other, own, head_ref, s_in, s_ref)


def first_scores_kernel(own, other, head_ref, s_in, s_ref):
    both_scores((0,), (own,), (other,), head_ref, s_in, s_ref)


def own_scores_kernel(a1, a2, a3, head_ref, s_in, s_ref):
    both_scores((1, 2, 3), (a1, a2, a3), None, head_ref, s_in, s_ref)


def last_scores_kernel(a1, a2, a3, head_ref, s_in, hit_ref, s_ref, stat_ref, ss):
    both_scores((1, 2, 3), None, (a1, a2, a3), head_ref, s_in, s_ref)

    def rows(i, _):
        at = pl.ds(pl.multiple_of(i * 32, 32), 32)
        s = s_ref[at, :]
        m = jnp.max(s, axis=1, keepdims=True)
        ss[at, 0:1] = m
        ss[at, 1:2] = jnp.sum(jnp.exp(s - m), axis=1, keepdims=True)
        ss[at, 2:3] = jnp.sum(jnp.where(hit_ref[at, :].astype(F32) > 0.5, s, 0.0), axis=1, keepdims=True)
        return _

    lax.fori_loop(0, 16, rows, 0)
    flat_stats = jnp.transpose(ss[...])
    for j in range(3):
        for k in range(4):
            stat_ref[j * 4 + k:j * 4 + k + 1, :] = flat_stats[j:j + 1, k * 128:(k + 1) * 128]
    stat_ref[12:16, :] = jnp.zeros((4, 128), F32)


def merge(a, b):
    m = jnp.maximum(a[0:4, :], b[0:4, :])
    total = a[4:8, :] * jnp.exp(a[0:4, :] - m) + b[4:8, :] * jnp.exp(b[0:4, :] - m)
    return m, total, a[8:12, :] + b[8:12, :]


def merge_kernel(a_ref, b_ref, out_ref):
    out_ref[0:4, :], out_ref[4:8, :], out_ref[8:12, :] = merge(a_ref, b_ref)
    out_ref[12:16, :] = jnp.zeros((4, 128), F32)


def residual_kernel(s_ref, hit_ref, a_ref, b_ref, res_ref, lp_ref, cs, lps):
    x, z, y, c = coords()
    m, total, picked = merge(a_ref, b_ref)
    lps[0:4, :] = picked - m - jnp.log(total)
    mine = lps[pl.ds(x, 1), :]
    mine = pltpu.roll(mine, (128 - 32 * z) & 127, 1)
    lp_ref[...] = mine[:, 0:32]
    for k in range(4):
        cs[k * 128:(k + 1) * 128, 0:128] = jnp.transpose(jnp.broadcast_to(m[k:k + 1, :], (128, 128)))
        cs[k * 128:(k + 1) * 128, 128:256] = jnp.transpose(jnp.broadcast_to(total[k:k + 1, :], (128, 128)))

    def rows(i, _):
        at = pl.ds(pl.multiple_of(i * 32, 32), 32)
        p = jnp.exp(s_ref[at, :] - cs[at, 0:1]) / cs[at, 128:129]
        res_ref[at, :] = (hit_ref[at, :].astype(F32) - p).astype(BF)
        return _

    lax.fori_loop(0, 16, rows, 0)


def block_products(ds, core, res_ref, head_ref, got, outs):
    x, z, y, c = coords()

    def put(i, q, v):
        if got is not None:
            v = v + got[i][q].astype(F32)
        outs[i][q] = v.astype(outs[i].dtype)

    @pl.when(core == 0)
    def _():
        for i, d in enumerate(ds):
            v = jnp.dot(res_ref[...], head_ref[:, features((y + d) & 3, 0)], preferred_element_type=F32)
            for q in range(4):
                put(i, q, v[q * 128:(q + 1) * 128])

    @pl.when(core == 1)
    def _():
        rows = [res_ref[pl.ds(pl.multiple_of(((x + d) & 3) * 128, 128), 128), :] for d in ds]
        rows = jnp.concatenate(rows, axis=0)
        for q in range(4):
            v = jnp.dot(rows, head_ref[:, features(q, 1)], preferred_element_type=F32)
            for i in range(len(ds)):
                put(i, q, v[i * 128:(i + 1) * 128])


def send_products_kernel(ds, res_ref, head_ref, *outs):
    block_products(ds, 1 - coords()[3], res_ref, head_ref, None, outs)


def keep_products_kernel(ds, res_ref, head_ref, *refs):
    block_products(ds, coords()[3], res_ref, head_ref, refs[:len(ds)], refs[len(ds):])


def ring_sum_kernel(own_in, r1, r2, r3, own_ref, b1, b2, b3):
    x, z, y, c = coords()
    own = jnp.where(c == 0, x, y)
    for d, out in enumerate((own_ref, b1, b2, b3)):
        q = (own + d) & 3
        v = own_in[q].astype(F32) + r1[q].astype(F32) + r2[q].astype(F32) + r3[q].astype(F32)
        out[...] = v.astype(out.dtype)


def return_kernel(rc_ref, own_in, r1, r2, r3, out_ref):
    v = (own_in[...] + r1[...] + r2[...] + r3[...]).astype(BF)
    sel = placing(rc_ref, (256, 128), 0, 16)
    out_ref[...] = jnp.dot(sel, v, preferred_element_type=F32).astype(BF)


def slots_kernel(rc_ref, cot_ref, arr_ref, out_ref):
    dp = lax.axis_index("dp")
    start, count = my_start(rc_ref, dp), rc_ref[dp]
    j, k = iota((64, 256), 0), iota((64, 256), 1)
    a = (start + j) & 15
    sel = ((k >> 6) == (a >> 2)) & (((k >> 2) & 3) == (j >> 4)) & ((k & 3) == (a & 3)) & (j < count)
    v = jnp.dot(sel.astype(F32).astype(BF), arr_ref[...], preferred_element_type=F32)
    g = start + iota((64, 512), 0)
    here = iota((64, 512), 1) == (g & 15) * 32 + (g >> 4)
    cot = jnp.sum(jnp.where(here, cot_ref[...], 0.0), axis=1, keepdims=True)
    out_ref[...] = (v * cot).astype(BF)


def sds(shape, dtype):
    return jax.ShapeDtypeStruct(shape, dtype)


def call(kernel, ins, outs, in_specs=None, scratch=(), limit=16, cost=None, aliases=None):
    multi = isinstance(outs, (list, tuple))
    return pl.pallas_call(
        kernel,
        out_shape=outs,
        in_specs=in_specs or [VM] * len(ins),
        out_specs=[VM] * len(outs) if multi else VM,
        scratch_shapes=list(scratch),
        compiler_params=params(limit),
        cost_estimate=cost,
        input_output_aliases=aliases or {},
    )(*ins)


def cost(flops, nbytes):
    return pl.CostEstimate(flops=flops, bytes_accessed=nbytes, transcendentals=0)


def per_device(hidden, head, row_counts, token_ids, segment_ids, cotangent):
    cols = head.shape[1]
    head = head.T
    outgoing = call(
        pack_kernel,
        (row_counts, hidden, token_ids.reshape(1, 32), segment_ids.reshape(1, 32), cotangent.reshape(1, 32)),
        sds((N_DP, 24, FEAT), BF),
        in_specs=[HBM] * 5,
        scratch=[
            pltpu.SMEM((16,), I32),
            pltpu.VMEM((64, FEAT), BF),
            pltpu.VMEM((1, 32), I32),
            pltpu.VMEM((1, 32), I32),
            pltpu.VMEM((1, 32), F32),
            pltpu.SemaphoreType.DMA((5,)),
        ],
    )
    arrived = lax.all_to_all(outgoing, "dp", 0, 0, tiled=True)
    g1 = call(unpack_kernel, (row_counts, arrived.reshape(384, FEAT)), sds((128, FEAT), BF), in_specs=[SM, VM])
    digits = arrived[:, 16:24, 0:32].astype(F32)
    tokens = (digits[:, 0] + 256.0 * digits[:, 1] + 65536.0 * digits[:, 2]).astype(I32).reshape(1, 512)
    segments = digits[:, 3].astype(I32).reshape(1, 512)
    cots = (digits[:, 4] + digits[:, 5] + digits[:, 6]).reshape(1, 512)

    second = [g1] + [permute(g1, shift_perm("xy", 4 - d)) for d in (1, 2, 3)]
    hits, s = call(
        functools.partial(code_kernel, cols),
        (tokens, segments),
        [sds((512, cols), BF), sds((512, cols), F32)],
        cost=cost(1 << 20, 1 << 10),
    )
    second, s = lax.optimization_barrier((second, s))
    g2 = call(place_kernel, second, sds((4, 128, FEAT), BF))
    third = [g2] + [permute(g2, shift_perm("yx", 4 - d)) for d in (1, 2, 3)]

    wide = sds((512, cols), F32)
    small = cost(1 << 20, 1 << 10)
    other = permute(g2, CORE_PERM)
    s = call(first_scores_kernel, (g2, other, head, s), wide, cost=small, aliases={3: 0})
    *third, s = lax.optimization_barrier((*third[1:], s))
    other = [permute(v, CORE_PERM) for v in third]
    s = call(own_scores_kernel, (*third, head, s), wide, cost=small, aliases={4: 0})
    s, stats = call(
        last_scores_kernel,
        (*other, head, s, hits),
        [wide, sds((16, 128), F32)],
        scratch=[pltpu.VMEM((512, 128), F32)],
        aliases={4: 0},
    )
    steps = [CORE_PERM] + [pairing(ax, b) for ax in "yxz" for b in (1, 3)]
    for i, pairs in enumerate(steps):
        got_stats = permute(stats, pairs)
        if i < 6:
            stats = call(merge_kernel, (stats, got_stats), sds((16, 128), F32))

    res, logprobs = call(
        residual_kernel,
        (s, hits, stats, got_stats),
        [sds((512, cols), BF), sds((1, 32), F32)],
        scratch=[pltpu.VMEM((512, 256), F32), pltpu.VMEM((8, 128), F32)],
    )
    quarter = sds((4, 128, FEAT), BF)
    got, ring = {}, {}
    pairs = ((1, 3), (2, 0))
    for ds in pairs:
        out = call(functools.partial(send_products_kernel, ds), (res, head), [quarter] * 2, cost=small)
        for d, v in zip(ds, out):
            got[d] = permute(v, CORE_PERM)
        res, _ = lax.optimization_barrier((res, out[0]))
    for ds in pairs:
        out = [quarter if d else sds((4, 128, FEAT), F32) for d in ds]
        out = call(functools.partial(keep_products_kernel, ds), (res, head, *[got[d] for d in ds]), out, cost=small)
        for d, v in zip(ds, out):
            ring[d] = permute(v, shift_perm("yx", d)) if d else v
        res, _ = lax.optimization_barrier((res, out[0]))
    own, *out = call(ring_sum_kernel, [ring[d] for d in range(4)], [sds((128, FEAT), F32)] * 4)
    ring = [permute(v, shift_perm("xy", d + 1)) for d, v in enumerate(out)]
    returning = call(
        return_kernel, (row_counts, own, *ring), sds((256, FEAT), BF), in_specs=[SM] + [VM] * 4
    )
    returned = lax.all_to_all(returning.reshape(N_DP, 16, FEAT), "dp", 0, 0, tiled=True)
    grad_hidden = call(
        slots_kernel, (row_counts, cots, returned.reshape(256, FEAT)), sds((64, FEAT), BF), in_specs=[SM, VM, VM]
    )
    return logprobs.reshape(32), grad_hidden


def solution(mesh):
    return jax.shard_map(
        per_device,
        mesh=mesh,
        in_specs=(P("dp", "vocab"), P(None, ("dp", "vocab")), P(), P("dp"), P("dp"), P("dp")),
        out_specs=(P("dp"), P("dp", "vocab")),
        check_vma=False,
    )
```

```python
import functools

import jax
import jax.numpy as jnp
from jax import lax
from jax.experimental import pallas as pl
from jax.experimental.pallas import tpu as pltpu
from jax.sharding import PartitionSpec as P

freq_weight = 0.4
presence_weight = 0.8

N_DP, N_VOC = 16, 8
FEAT = 512
BF, F32, I32 = jnp.bfloat16, jnp.float32, jnp.int32
MIB = 1 << 20


def params(limit=32):
    return pltpu.CompilerParams(vmem_limit_bytes=limit * MIB)


def coords():
    dp, voc = lax.axis_index("dp"), lax.axis_index("vocab")
    return dp // 4, lax.rem(dp, 4), voc // 2, lax.rem(voc, 2)


def flat(x, z, y, c):
    return x * 32 + z * 8 + y * 2 + c


def shift_perm(axes, k):
    pairs = []
    for x in range(4):
        for z in range(4):
            for y in range(4):
                for c in range(2):
                    to = dict(x=x, z=z, y=y, c=c)
                    to[axes[c]] = (to[axes[c]] + k) % 4
                    pairs.append((flat(x, z, y, c), flat(**to)))
    return pairs


def pairing(axis, bits, cores=(0, 1)):
    pairs = []
    for x in range(4):
        for z in range(4):
            for y in range(4):
                for c in cores:
                    to = dict(x=x, z=z, y=y, c=c)
                    to[axis] ^= bits
                    pairs.append((flat(x, z, y, c), flat(**to)))
    return pairs


CORE_PERM = [(i, i ^ 1) for i in range(N_DP * N_VOC)]


def permute(v, pairs):
    return lax.ppermute(v, ("dp", "vocab"), pairs)


def iota(shape, dim):
    return lax.broadcasted_iota(I32, shape, dim)


VM = pl.BlockSpec(memory_space=pltpu.VMEM)
SM = pl.BlockSpec(memory_space=pltpu.SMEM)
HBM = pl.BlockSpec(memory_space=pltpu.HBM)


def my_start(rc_ref, dp):
    start = jnp.int32(0)
    for s in range(N_DP):
        start = start + jnp.where(s < dp, rc_ref[s], 0)
    return start


def pack_kernel(meta_ref, hid_ref, out_ref):
    dp = lax.axis_index("dp")
    counts = meta_ref[:, 0:16]
    lane = iota((1, 16), 1)
    start = jnp.sum(jnp.where(lane < dp, counts, 0.0), axis=1, keepdims=True).astype(I32)
    count = jnp.sum(jnp.where(lane == dp, counts, 0.0), axis=1, keepdims=True).astype(I32)
    row, col = iota((64, 64), 0), iota((64, 64), 1)
    target = (row >> 4) * 4 + (row & 3)
    src = ((row >> 2) & 3) * N_DP + ((target - start) & 15)
    sel = (col == src) & (col < count)
    rows = jnp.dot(sel.astype(F32).astype(BF), hid_ref[...], preferred_element_type=F32).astype(BF)
    kind = iota((8, 32), 0)
    tok = meta_ref[:, 16:48].astype(I32)
    cot = meta_ref[:, 80:112]
    digit = jnp.where(kind == 0, tok & 255, jnp.where(kind == 1, (tok >> 8) & 255, tok >> 16)).astype(F32)
    digit = jnp.where(kind == 3, meta_ref[:, 48:80], digit)
    high = cot.astype(BF).astype(F32)
    mid = (cot - high).astype(BF).astype(F32)
    low = cot - high - mid
    digit = jnp.where(kind < 4, digit, jnp.where(kind == 4, high, jnp.where(kind == 5, mid, low))).astype(BF)
    for a in range(N_DP):
        out_ref[a, 0:16, :] = rows[(a // 4) * 16:(a // 4) * 16 + 16]
        out_ref[a, 16:24, :] = jnp.zeros((8, FEAT), BF)
        out_ref[a, 16:24, 0:32] = digit


def placing(rc_ref, shape, slot_dim, per_source):
    x = lax.axis_index("dp") // 4
    k, row = iota(shape, slot_dim), iota(shape, 1 - slot_dim)
    s = k >> 4 if per_source == 16 else (k * 2731) >> 16
    u = k - s * per_source
    t, z = u >> 2, u & 3
    start = jnp.zeros(shape, I32)
    count = jnp.zeros(shape, I32)
    run = jnp.int32(0)
    for i in range(N_DP):
        start = jnp.where(s == i, run, start)
        count = jnp.where(s == i, rc_ref[i], count)
        run = run + rc_ref[i]
    a = x * 4 + z
    offset = (a - start) & 15
    base = (start + offset - a) >> 4
    sel = (u < 16) & (t * N_DP + offset < count) & (z * 32 + base + t == row)
    return sel.astype(F32).astype(BF)


def unpack_kernel(rc_ref, arr_ref, out_ref):
    sel = placing(rc_ref, (128, 384), 1, 24)
    out_ref[...] = jnp.dot(sel, arr_ref[...], preferred_element_type=F32).astype(BF)


def place_kernel(a0, a1, a2, a3, out_ref):
    x, z, y, c = coords()
    own = jnp.where(c == 0, x, y)
    for d, a in enumerate((a0, a1, a2, a3)):
        out_ref[pl.ds((own + d) & 3, 1)] = a[...][None]


def column(row):
    wide = jnp.broadcast_to(row, (128, row.shape[1]))
    return jnp.transpose(wide)[:, 0:1]


def code_kernel(cols, tok_ref, seg_ref, hit_ref, start_ref):
    dp, voc = lax.axis_index("dp"), lax.axis_index("vocab")
    tok, seg = tok_ref[...], seg_ref[...]
    tok_col = column(tok.astype(F32)).astype(I32)
    seg_col = column(seg.astype(F32)).astype(I32)
    prior = (seg_col == seg) & (iota((512, 512), 1) < iota((512, 512), 0))
    prior = prior.astype(F32).astype(BF)
    first = (dp * N_VOC + voc) * cols
    hits = (tok_col == first + iota((512, cols), 1)).astype(F32).astype(BF)
    hit_ref[...] = hits
    counts = jnp.dot(prior, hits, preferred_element_type=F32)
    start_ref[...] = -(freq_weight * counts) - presence_weight * (counts > 0).astype(F32)


def features(yy, core):
    return pl.ds(pl.multiple_of((yy * 2 + core) * FEAT, FEAT), FEAT)


def block_scores(ds, zero, one, head_ref, s_in, s_ref):
    x, z, y, c = coords()
    dims = (((1,), (1,)), ((), ()))
    if zero is not None:
        part = s_in[...]
        for d, block in zip(ds, zero):
            w = head_ref[:, features((y + d) & 3, 0)]
            part += lax.dot_general(block[...].reshape(512, FEAT), w, dims, preferred_element_type=F32)
        s_ref[...] = part
    else:
        s_ref[...] = s_in[...]
    if one is not None:
        part = None
        for q in range(4):
            rows = jnp.concatenate([block[q] for block in one], axis=0)
            v = lax.dot_general(rows, head_ref[:, features(q, 1)], dims, preferred_element_type=F32)
            part = v if part is None else part + v
        for i, d in enumerate(ds):
            s_ref[pl.ds(pl.multiple_of(((x + d) & 3) * 128, 128), 128), :] += part[i * 128:(i + 1) * 128]


def both_scores(ds, own, other, head_ref, s_in, s_ref):
    c = coords()[3]

    @pl.when(c == 0)
    def _():
        block_scores(ds, own, other, head_ref, s_in, s_ref)

    @pl.when(c == 1)
    def _():
        block_scores(ds, other, own, head_ref, s_in, s_ref)


def first_scores_kernel(own, other, head_ref, s_in, s_ref):
    both_scores((0,), (own,), (other,), head_ref, s_in, s_ref)


def own_scores_kernel(a1, a2, a3, head_ref, s_in, s_ref):
    both_scores((1, 2, 3), (a1, a2, a3), None, head_ref, s_in, s_ref)


def last_scores_kernel(a1, a2, a3, head_ref, s_in, hit_ref, s_ref, exp_ref, stat_ref, ss):
    both_scores((1, 2, 3), None, (a1, a2, a3), head_ref, s_in, s_ref)

    def rows(i, _):
        at = pl.ds(pl.multiple_of(i * 32, 32), 32)
        s = s_ref[at, :]
        hit = hit_ref[at, :].astype(F32) > 0.5
        m = jnp.max(s, axis=1, keepdims=True)
        e = jnp.exp(s - m)
        exp_ref[at, :] = jnp.where(hit, 0.0, e).astype(BF)
        ss[at, 0:1] = m
        ss[at, 1:2] = jnp.sum(e, axis=1, keepdims=True)
        ss[at, 2:3] = jnp.sum(jnp.where(hit, s, 0.0), axis=1, keepdims=True)
        return _

    lax.fori_loop(0, 16, rows, 0, unroll=4)
    flat_stats = jnp.transpose(ss[...])
    for j in range(3):
        for k in range(4):
            piece = flat_stats[j:j + 1, k * 128:(k + 1) * 128]
            for n in range(N_VOC):
                stat_ref[n, j * 4 + k:j * 4 + k + 1, :] = piece
    for n in range(N_VOC):
        stat_ref[n, 12:16, :] = jnp.zeros((4, 128), F32)


def merge(st_ref, n):
    m = st_ref[0, 0:4, :]
    for i in range(1, n):
        m = jnp.maximum(m, st_ref[i, 0:4, :])
    total = jnp.zeros_like(m)
    picked = jnp.zeros_like(m)
    for i in range(n):
        total = total + st_ref[i, 4:8, :] * jnp.exp(st_ref[i, 0:4, :] - m)
        picked = picked + st_ref[i, 8:12, :]
    return m, total, picked


def merge_kernel(st_ref, out_ref, chip_ref):
    voc = lax.axis_index("vocab")
    m, total, picked = merge(st_ref, N_VOC)
    for n in range(N_DP):
        out_ref[n, 0:4, :] = m
        out_ref[n, 4:8, :] = total
        out_ref[n, 8:12, :] = picked
        out_ref[n, 12:16, :] = jnp.zeros((4, 128), F32)
    chip_ref[0:4, :] = st_ref[voc, 0:4, :]
    chip_ref[4:8, :] = st_ref[voc ^ 1, 0:4, :]


def long_row(v):
    return jnp.concatenate([v[k:k + 1, :] for k in range(4)], axis=1)


def columns(rows, out_ref):
    place = iota((128, rows[0].shape[1]), 0)
    wide = jnp.zeros(place.shape, F32)
    for i, row in enumerate(rows):
        wide = jnp.where(place == i, row, wide)
    out_ref[...] = jnp.transpose(wide)


def factor_kernel(st_ref, chip_ref, factor_ref, lp_ref, lps):
    x, z, y, c = coords()
    m, total, picked = merge(st_ref, N_DP)
    lps[0:4, :] = picked - m - jnp.log(total)
    mine = pltpu.roll(lps[pl.ds(x, 1), :], (128 - 32 * z) & 127, 1)
    lp_ref[...] = mine[:, 0:32]
    own, other = (jnp.exp(chip_ref[i:i + 4, :] - m) / total for i in (0, 4))
    columns([long_row(v) for v in (own, other, 1.0 - jnp.exp(picked - m) / total)], factor_ref)


def block_products(ds, core, left_ref, head_ref, put):
    x, z, y, c = coords()

    @pl.when(core == 0)
    def _():
        for i, d in enumerate(ds):
            v = jnp.dot(left_ref[...], head_ref[:, features((y + d) & 3, 0)], preferred_element_type=F32)
            for q in range(4):
                put(i, q, q * 128, v[q * 128:(q + 1) * 128])

    @pl.when(core == 1)
    def _():
        ats = [pl.multiple_of(((x + d) & 3) * 128, 128) for d in ds]
        rows = jnp.concatenate([left_ref[pl.ds(at, 128), :] for at in ats], axis=0)
        for q in range(4):
            v = jnp.dot(rows, head_ref[:, features(q, 1)], preferred_element_type=F32)
            for i, at in enumerate(ats):
                put(i, q, at, v[i * 128:(i + 1) * 128])


def send_products_kernel(ds, left_ref, head_ref, *outs):
    def put(i, q, at, v):
        outs[i][q] = v.astype(BF)

    block_products(ds, 1 - coords()[3], left_ref, head_ref, put)


def target_products_kernel(left_ref, head_ref, send_ref, keep_ref):
    c = coords()[3]
    for core, out in ((1 - c, send_ref), (c, keep_ref)):
        def put(i, q, at, v, out=out):
            out[i, q] = v.astype(BF)

        block_products((0, 1, 2, 3), core, left_ref, head_ref, put)


def combine_kernel(ds, left_ref, head_ref, factor_ref, tk_ref, tg_ref, *refs):
    got, outs = refs[:len(ds)], refs[len(ds):]

    def put(i, q, at, v):
        f = factor_ref[pl.ds(at, 128), :]
        target = tk_ref[ds[i], q].astype(F32) + tg_ref[ds[i], q].astype(F32)
        v = target * f[:, 2:3] - (v * f[:, 0:1] + got[i][q].astype(F32) * f[:, 1:2])
        outs[i][q] = v.astype(outs[i].dtype)

    block_products(ds, coords()[3], left_ref, head_ref, put)


def ring_sum_kernel(own_in, r1, r2, r3, own_ref, b1, b2, b3):
    x, z, y, c = coords()
    own = jnp.where(c == 0, x, y)
    for d, out in enumerate((own_ref, b1, b2, b3)):
        q = (own + d) & 3
        out[...] = own_in[q] + r1[q].astype(F32) + r2[q].astype(F32) + r3[q].astype(F32)


def ways_kernel(rc_ref, cot_ref, back_ref, slot_ref, weight_ref):
    back_ref[...] = placing(rc_ref, (256, 128), 0, 16)
    dp = lax.axis_index("dp")
    start, count = my_start(rc_ref, dp), rc_ref[dp]
    j, k = iota((64, 256), 0), iota((64, 256), 1)
    a = (start + j) & 15
    sel = ((k >> 6) == (a >> 2)) & (((k >> 2) & 3) == (j >> 4)) & ((k & 3) == (a & 3)) & (j < count)
    slot_ref[...] = sel.astype(F32).astype(BF)
    g = start + iota((64, 512), 0)
    here = iota((64, 512), 1) == (g & 15) * 32 + (g >> 4)
    cot = jnp.sum(jnp.where(here, cot_ref[...], 0.0), axis=1, keepdims=True)
    weight_ref[...] = jnp.broadcast_to(cot, (64, 128))


def return_kernel(back_ref, own_in, r1, r2, r3, out_ref):
    v = (own_in[...] + r1[...] + r2[...] + r3[...]).astype(BF)
    out_ref[...] = jnp.dot(back_ref[...], v, preferred_element_type=F32).astype(BF)


def slots_kernel(slot_ref, weight_ref, arr_ref, out_ref):
    v = jnp.dot(slot_ref[...], arr_ref[...], preferred_element_type=F32)
    out_ref[...] = (v * weight_ref[:, 0:1]).astype(BF)


def sds(shape, dtype):
    return jax.ShapeDtypeStruct(shape, dtype)


def call(kernel, ins, outs, in_specs=None, scratch=(), limit=12, cost=None, aliases=None):
    multi = isinstance(outs, (list, tuple))
    return pl.pallas_call(
        kernel,
        out_shape=outs,
        in_specs=in_specs or [VM] * len(ins),
        out_specs=[VM] * len(outs) if multi else VM,
        scratch_shapes=list(scratch),
        compiler_params=params(limit),
        cost_estimate=cost,
        input_output_aliases=aliases or {},
    )(*ins)


def cost(flops, nbytes):
    return pl.CostEstimate(flops=flops, bytes_accessed=nbytes, transcendentals=0)


def per_device(hidden, head, row_counts, token_ids, segment_ids, cotangent):
    cols = head.shape[1]
    head = head.T
    meta = jnp.pad(row_counts, (0, 96)) + jnp.pad(token_ids, (16, 64)) + jnp.pad(segment_ids, (48, 32))
    meta = meta.astype(F32) + jnp.pad(cotangent, (80, 0))
    outgoing = call(pack_kernel, (meta.reshape(1, 112), hidden), sds((N_DP, 24, FEAT), BF))
    arrived = lax.all_to_all(outgoing, "dp", 0, 0, tiled=True)
    g1 = call(unpack_kernel, (row_counts, arrived.reshape(384, FEAT)), sds((128, FEAT), BF), in_specs=[SM, VM])
    digits = arrived[:, 16:24, 0:32].astype(F32)
    tokens = (digits[:, 0] + 256.0 * digits[:, 1] + 65536.0 * digits[:, 2]).astype(I32).reshape(1, 512)
    segments = digits[:, 3].astype(I32).reshape(1, 512)
    cots = (digits[:, 4] + digits[:, 5] + digits[:, 6]).reshape(1, 512)

    second = [g1] + [permute(g1, shift_perm("xy", 4 - d)) for d in (1, 2, 3)]
    hits, s = call(
        functools.partial(code_kernel, cols),
        (tokens, segments),
        [sds((512, cols), BF), sds((512, cols), F32)],
        cost=cost(1 << 20, 1 << 10),
    )
    second, s = lax.optimization_barrier((second, s))
    g2 = call(place_kernel, second, sds((4, 128, FEAT), BF))
    third = [g2] + [permute(g2, shift_perm("yx", 4 - d)) for d in (1, 2, 3)]

    wide = sds((512, cols), F32)
    small = cost(1 << 20, 1 << 10)
    quarter = sds((4, 128, FEAT), BF)
    pairs = ((1, 3), (2, 0))
    target_send, target_keep = call(
        target_products_kernel, (hits, head), [sds((4, 4, 128, FEAT), BF)] * 2, cost=small
    )
    other = permute(g2, CORE_PERM)
    s = call(first_scores_kernel, (g2, other, head, s), wide, cost=small, aliases={3: 0})
    *third, s, target_keep = lax.optimization_barrier((*third[1:], s, target_keep))
    other = [permute(v, CORE_PERM) for v in third]
    s = call(own_scores_kernel, (*third, head, s), wide, cost=small, aliases={4: 0})
    _, exps, stats = call(
        last_scores_kernel,
        (*other, head, s, hits),
        [wide, sds((512, cols), BF), sds((N_VOC, 16, 128), F32)],
        scratch=[pltpu.VMEM((512, 128), F32)],
        aliases={4: 0},
    )
    stats = lax.all_to_all(stats, "vocab", 0, 0, tiled=True)
    stats, chip = call(merge_kernel, (stats,), [sds((N_DP, 16, 128), F32), sds((8, 128), F32)])
    exps, chip, target_send = lax.optimization_barrier((exps, chip, target_send))
    target_got = permute(target_send, CORE_PERM)
    stats = lax.all_to_all(stats, "dp", 0, 0, tiled=True)
    got = {}
    for ds in pairs:
        out = call(functools.partial(send_products_kernel, ds), (exps, head), [quarter] * 2, cost=small)
        for d, v in zip(ds, out):
            got[d] = permute(v, CORE_PERM)
    factors, logprobs = call(
        factor_kernel, (stats, chip), [sds((512, 128), F32), sds((1, 32), F32)], scratch=[pltpu.VMEM((8, 128), F32)],
    )
    ring = {}
    for ds in pairs:
        out = call(
            functools.partial(combine_kernel, ds),
            (exps, head, factors, target_keep, target_got, *[got[d] for d in ds]),
            [quarter if d else sds((4, 128, FEAT), F32) for d in ds],
            cost=small,
        )
        for d, v in zip(ds, out):
            ring[d] = permute(v, shift_perm("yx", d)) if d else v
        factors, _ = lax.optimization_barrier((factors, out[0]))
    own, *out = call(ring_sum_kernel, [ring[d] for d in range(4)], [sds((128, FEAT), F32)] * 4)
    ring = [own] + [permute(v, shift_perm("xy", d + 1)) for d, v in enumerate(out)]
    back, slot, weight = call(
        ways_kernel,
        (row_counts, cots),
        [sds((256, 128), BF), sds((64, 256), BF), sds((64, 128), F32)],
        in_specs=[SM, VM],
        cost=small,
    )
    returning = call(return_kernel, (back, *ring), sds((256, FEAT), BF))
    returned = lax.all_to_all(returning.reshape(N_DP, 16, FEAT), "dp", 0, 0, tiled=True)
    grad_hidden = call(slots_kernel, (slot, weight, returned.reshape(256, FEAT)), sds((64, FEAT), BF))
    return logprobs.reshape(32), grad_hidden


def solution(mesh):
    return jax.shard_map(
        per_device,
        mesh=mesh,
        in_specs=(P("dp", "vocab"), P(None, ("dp", "vocab")), P(), P("dp"), P("dp"), P("dp")),
        out_specs=(P("dp"), P("dp", "vocab")),
        check_vma=False,
    )
```

```python
import functools

import jax
import jax.numpy as jnp
from jax import lax
from jax.experimental import pallas as pl
from jax.experimental.pallas import tpu as pltpu
from jax.sharding import PartitionSpec as P

freq_weight = 0.4
presence_weight = 0.8

N_DP, N_VOC = 16, 8
FEAT = 512
BF, F32, I32 = jnp.bfloat16, jnp.float32, jnp.int32
MIB = 1 << 20


def params(limit=32):
    return pltpu.CompilerParams(vmem_limit_bytes=limit * MIB)


def coords():
    dp, voc = lax.axis_index("dp"), lax.axis_index("vocab")
    return dp // 4, lax.rem(dp, 4), voc // 2, lax.rem(voc, 2)


def flat(x, z, y, c):
    return x * 32 + z * 8 + y * 2 + c


def shift_perm(axes, k):
    pairs = []
    for x in range(4):
        for z in range(4):
            for y in range(4):
                for c in range(2):
                    to = dict(x=x, z=z, y=y, c=c)
                    to[axes[c]] = (to[axes[c]] + k) % 4
                    pairs.append((flat(x, z, y, c), flat(**to)))
    return pairs


def pairing(axis, bits, cores=(0, 1)):
    pairs = []
    for x in range(4):
        for z in range(4):
            for y in range(4):
                for c in cores:
                    to = dict(x=x, z=z, y=y, c=c)
                    to[axis] ^= bits
                    pairs.append((flat(x, z, y, c), flat(**to)))
    return pairs


CORE_PERM = [(i, i ^ 1) for i in range(N_DP * N_VOC)]


def permute(v, pairs):
    return lax.ppermute(v, ("dp", "vocab"), pairs)


def iota(shape, dim):
    return lax.broadcasted_iota(I32, shape, dim)


VM = pl.BlockSpec(memory_space=pltpu.VMEM)
SM = pl.BlockSpec(memory_space=pltpu.SMEM)
HBM = pl.BlockSpec(memory_space=pltpu.HBM)


def my_start(rc_ref, dp):
    start = jnp.int32(0)
    for s in range(N_DP):
        start = start + jnp.where(s < dp, rc_ref[s], 0)
    return start


def pack_kernel(meta_ref, hid_ref, out_ref):
    dp = lax.axis_index("dp")
    counts = meta_ref[:, 0:16]
    lane = iota((1, 16), 1)
    start = jnp.sum(jnp.where(lane < dp, counts, 0.0), axis=1, keepdims=True).astype(I32)
    count = jnp.sum(jnp.where(lane == dp, counts, 0.0), axis=1, keepdims=True).astype(I32)
    row, col = iota((64, 64), 0), iota((64, 64), 1)
    target = (row >> 4) * 4 + (row & 3)
    src = ((row >> 2) & 3) * N_DP + ((target - start) & 15)
    sel = (col == src) & (col < count)
    rows = jnp.dot(sel.astype(F32).astype(BF), hid_ref[...], preferred_element_type=F32).astype(BF)
    kind = iota((8, 32), 0)
    tok = meta_ref[:, 16:48].astype(I32)
    cot = meta_ref[:, 80:112]
    digit = jnp.where(kind == 0, tok & 255, jnp.where(kind == 1, (tok >> 8) & 255, tok >> 16)).astype(F32)
    digit = jnp.where(kind == 3, meta_ref[:, 48:80], digit)
    high = cot.astype(BF).astype(F32)
    mid = (cot - high).astype(BF).astype(F32)
    low = cot - high - mid
    digit = jnp.where(kind < 4, digit, jnp.where(kind == 4, high, jnp.where(kind == 5, mid, low))).astype(BF)
    for a in range(N_DP):
        out_ref[a, 0:16, :] = rows[(a // 4) * 16:(a // 4) * 16 + 16]
        out_ref[a, 16:24, :] = jnp.zeros((8, FEAT), BF)
        out_ref[a, 16:24, 0:32] = digit


def placing(rc_ref, shape, slot_dim, per_source):
    x = lax.axis_index("dp") // 4
    k, row = iota(shape, slot_dim), iota(shape, 1 - slot_dim)
    s = k >> 4 if per_source == 16 else (k * 2731) >> 16
    u = k - s * per_source
    t, z = u >> 2, u & 3
    start = jnp.zeros(shape, I32)
    count = jnp.zeros(shape, I32)
    run = jnp.int32(0)
    for i in range(N_DP):
        start = jnp.where(s == i, run, start)
        count = jnp.where(s == i, rc_ref[i], count)
        run = run + rc_ref[i]
    a = x * 4 + z
    offset = (a - start) & 15
    base = (start + offset - a) >> 4
    sel = (u < 16) & (t * N_DP + offset < count) & (z * 32 + base + t == row)
    return sel.astype(F32).astype(BF)


def unpack_kernel(rc_ref, arr_ref, out_ref):
    sel = placing(rc_ref, (128, 384), 1, 24)
    out_ref[...] = jnp.dot(sel, arr_ref[...], preferred_element_type=F32).astype(BF)


def place_kernel(a0, a1, a2, a3, out_ref):
    x, z, y, c = coords()
    own = jnp.where(c == 0, x, y)
    for d, a in enumerate((a0, a1, a2, a3)):
        out_ref[pl.ds((own + d) & 3, 1)] = a[...][None]


def column(row):
    wide = jnp.broadcast_to(row, (128, row.shape[1]))
    return jnp.transpose(wide)[:, 0:1]


def code_kernel(cols, tok_ref, seg_ref, hit_ref, start_ref):
    dp, voc = lax.axis_index("dp"), lax.axis_index("vocab")
    tok, seg = tok_ref[...], seg_ref[...]
    tok_col = column(tok.astype(F32)).astype(I32)
    seg_col = column(seg.astype(F32)).astype(I32)
    prior = (seg_col == seg) & (iota((512, 512), 1) < iota((512, 512), 0))
    prior = prior.astype(F32).astype(BF)
    first = (dp * N_VOC + voc) * cols
    hits = (tok_col == first + iota((512, cols), 1)).astype(F32).astype(BF)
    hit_ref[...] = hits
    counts = jnp.dot(prior, hits, preferred_element_type=F32)
    start_ref[...] = -(freq_weight * counts) - presence_weight * (counts > 0).astype(F32)


def features(yy, core):
    return pl.ds(pl.multiple_of((yy * 2 + core) * FEAT, FEAT), FEAT)


def block_scores(ds, zero, one, head_ref, s_in, s_ref):
    x, z, y, c = coords()
    dims = (((1,), (1,)), ((), ()))
    if zero is not None:
        part = s_in[...]
        for d, block in zip(ds, zero):
            w = head_ref[:, features((y + d) & 3, 0)]
            part += lax.dot_general(block[...].reshape(512, FEAT), w, dims, preferred_element_type=F32)
        s_ref[...] = part
    else:
        s_ref[...] = s_in[...]
    if one is not None:
        def step(q, _):
            rows = jnp.concatenate([block[q] for block in one], axis=0)
            part = lax.dot_general(rows, head_ref[:, features(q, 1)], dims, preferred_element_type=F32)
            for i, d in enumerate(ds):
                s_ref[pl.ds(pl.multiple_of(((x + d) & 3) * 128, 128), 128), :] += part[i * 128:(i + 1) * 128]
            return _

        lax.fori_loop(0, 4, step, 0)


def both_scores(ds, own, other, head_ref, s_in, s_ref):
    c = coords()[3]

    @pl.when(c == 0)
    def _():
        block_scores(ds, own, other, head_ref, s_in, s_ref)

    @pl.when(c == 1)
    def _():
        block_scores(ds, other, own, head_ref, s_in, s_ref)


def first_scores_kernel(own, other, head_ref, s_in, s_ref):
    both_scores((0,), (own,), (other,), head_ref, s_in, s_ref)


def own_scores_kernel(a1, a2, a3, head_ref, s_in, s_ref):
    both_scores((1, 2, 3), (a1, a2, a3), None, head_ref, s_in, s_ref)


def last_scores_kernel(a1, a2, a3, head_ref, s_in, hit_ref, s_ref, exp_ref, stat_ref, ss):
    both_scores((1, 2, 3), None, (a1, a2, a3), head_ref, s_in, s_ref)

    def rows(i, _):
        at = pl.ds(pl.multiple_of(i * 32, 32), 32)
        s = s_ref[at, :]
        hit = hit_ref[at, :].astype(F32) > 0.5
        m = jnp.max(s, axis=1, keepdims=True)
        e = jnp.exp(s - m)
        exp_ref[at, :] = jnp.where(hit, 0.0, e).astype(BF)
        ss[at, 0:1] = m
        ss[at, 1:2] = jnp.sum(e, axis=1, keepdims=True)
        ss[at, 2:3] = jnp.sum(jnp.where(hit, s, 0.0), axis=1, keepdims=True)
        return _

    lax.fori_loop(0, 16, rows, 0, unroll=4)
    flat_stats = jnp.transpose(ss[...])
    for j in range(3):
        for k in range(4):
            piece = flat_stats[j:j + 1, k * 128:(k + 1) * 128]
            for n in range(N_VOC):
                stat_ref[n, j * 4 + k:j * 4 + k + 1, :] = piece
    for n in range(N_VOC):
        stat_ref[n, 12:16, :] = jnp.zeros((4, 128), F32)


def merge(st_ref, n):
    m = st_ref[0, 0:4, :]
    for i in range(1, n):
        m = jnp.maximum(m, st_ref[i, 0:4, :])
    total = jnp.zeros_like(m)
    picked = jnp.zeros_like(m)
    for i in range(n):
        total = total + st_ref[i, 4:8, :] * jnp.exp(st_ref[i, 0:4, :] - m)
        picked = picked + st_ref[i, 8:12, :]
    return m, total, picked


def merge_kernel(st_ref, out_ref, chip_ref):
    voc = lax.axis_index("vocab")
    m, total, picked = merge(st_ref, N_VOC)
    for n in range(N_DP):
        out_ref[n, 0:4, :] = m
        out_ref[n, 4:8, :] = total
        out_ref[n, 8:12, :] = picked
        out_ref[n, 12:16, :] = jnp.zeros((4, 128), F32)
    chip_ref[0:4, :] = st_ref[voc, 0:4, :]
    chip_ref[4:8, :] = st_ref[voc ^ 1, 0:4, :]


def long_row(v):
    return jnp.concatenate([v[k:k + 1, :] for k in range(4)], axis=1)


def columns(rows, out_ref):
    place = iota((128, rows[0].shape[1]), 0)
    wide = jnp.zeros(place.shape, F32)
    for i, row in enumerate(rows):
        wide = jnp.where(place == i, row, wide)
    out_ref[...] = jnp.transpose(wide)


def factor_kernel(st_ref, chip_ref, factor_ref, lp_ref, lps):
    x, z, y, c = coords()
    m, total, picked = merge(st_ref, N_DP)
    lps[0:4, :] = picked - m - jnp.log(total)
    mine = pltpu.roll(lps[pl.ds(x, 1), :], (128 - 32 * z) & 127, 1)
    lp_ref[...] = mine[:, 0:32]
    own, other = (jnp.exp(chip_ref[i:i + 4, :] - m) / total for i in (0, 4))
    columns([long_row(v) for v in (own, other, 1.0 - jnp.exp(picked - m) / total)], factor_ref)


def block_products(ds, core, left_ref, head_ref, put):
    x, z, y, c = coords()

    @pl.when(core == 0)
    def _():
        def one(i, d):
            v = jnp.dot(left_ref[...], head_ref[:, features((y + d) & 3, 0)], preferred_element_type=F32)
            for q in range(4):
                put(i, q, q * 128, v[q * 128:(q + 1) * 128])

        if ds == (0, 1, 2, 3):
            lax.fori_loop(0, 4, lambda d, _: one(d, d) or _, 0)
        else:
            for i, d in enumerate(ds):
                one(i, d)

    @pl.when(core == 1)
    def _():
        def step(q, _):
            ats = [pl.multiple_of(((x + d) & 3) * 128, 128) for d in ds]
            rows = jnp.concatenate([left_ref[pl.ds(at, 128), :] for at in ats], axis=0)
            v = jnp.dot(rows, head_ref[:, features(q, 1)], preferred_element_type=F32)
            for i, at in enumerate(ats):
                put(i, q, at, v[i * 128:(i + 1) * 128])
            return _

        lax.fori_loop(0, 4, step, 0)


def send_products_kernel(ds, left_ref, head_ref, *outs):
    def put(i, q, at, v):
        outs[i][q] = v.astype(BF)

    block_products(ds, 1 - coords()[3], left_ref, head_ref, put)


def target_products_kernel(left_ref, head_ref, send_ref, keep_ref):
    c = coords()[3]
    for core, out in ((1 - c, send_ref), (c, keep_ref)):
        def put(i, q, at, v, out=out):
            out[i, q] = v.astype(BF)

        block_products((0, 1, 2, 3), core, left_ref, head_ref, put)


def combine_kernel(ds, left_ref, head_ref, factor_ref, tk_ref, tg_ref, *refs):
    got, outs = refs[:len(ds)], refs[len(ds):]

    def put(i, q, at, v):
        f = factor_ref[pl.ds(at, 128), :]
        target = tk_ref[ds[i], q].astype(F32) + tg_ref[ds[i], q].astype(F32)
        v = target * f[:, 2:3] - (v * f[:, 0:1] + got[i][q].astype(F32) * f[:, 1:2])
        outs[i][q] = v.astype(outs[i].dtype)

    block_products(ds, coords()[3], left_ref, head_ref, put)


def ring_sum_kernel(own_in, r1, r2, r3, own_ref, b1, b2, b3):
    x, z, y, c = coords()
    own = jnp.where(c == 0, x, y)
    for d, out in enumerate((own_ref, b1, b2, b3)):
        q = (own + d) & 3
        out[...] = own_in[q] + r1[q].astype(F32) + r2[q].astype(F32) + r3[q].astype(F32)


def ways_kernel(rc_ref, cot_ref, back_ref, slot_ref, weight_ref):
    back_ref[...] = placing(rc_ref, (256, 128), 0, 16)
    dp = lax.axis_index("dp")
    start, count = my_start(rc_ref, dp), rc_ref[dp]
    j, k = iota((64, 256), 0), iota((64, 256), 1)
    a = (start + j) & 15
    sel = ((k >> 6) == (a >> 2)) & (((k >> 2) & 3) == (j >> 4)) & ((k & 3) == (a & 3)) & (j < count)
    slot_ref[...] = sel.astype(F32).astype(BF)
    g = start + iota((64, 512), 0)
    here = iota((64, 512), 1) == (g & 15) * 32 + (g >> 4)
    cot = jnp.sum(jnp.where(here, cot_ref[...], 0.0), axis=1, keepdims=True)
    weight_ref[...] = jnp.broadcast_to(cot, (64, 128))


def return_kernel(back_ref, own_in, r1, r2, r3, out_ref):
    v = (own_in[...] + r1[...] + r2[...] + r3[...]).astype(BF)
    out_ref[...] = jnp.dot(back_ref[...], v, preferred_element_type=F32).astype(BF)


def slots_kernel(slot_ref, weight_ref, arr_ref, out_ref):
    v = jnp.dot(slot_ref[...], arr_ref[...], preferred_element_type=F32)
    out_ref[...] = (v * weight_ref[:, 0:1]).astype(BF)


def sds(shape, dtype):
    return jax.ShapeDtypeStruct(shape, dtype)


def call(kernel, ins, outs, in_specs=None, scratch=(), limit=12, cost=None, aliases=None):
    multi = isinstance(outs, (list, tuple))
    return pl.pallas_call(
        kernel,
        out_shape=outs,
        in_specs=in_specs or [VM] * len(ins),
        out_specs=[VM] * len(outs) if multi else VM,
        scratch_shapes=list(scratch),
        compiler_params=params(limit),
        cost_estimate=cost,
        input_output_aliases=aliases or {},
    )(*ins)


def cost(flops, nbytes):
    return pl.CostEstimate(flops=flops, bytes_accessed=nbytes, transcendentals=0)


def per_device(hidden, head, row_counts, token_ids, segment_ids, cotangent):
    cols = head.shape[1]
    head = head.T
    meta = jnp.pad(row_counts, (0, 96)) + jnp.pad(token_ids, (16, 64)) + jnp.pad(segment_ids, (48, 32))
    meta = meta.astype(F32) + jnp.pad(cotangent, (80, 0))
    outgoing = call(pack_kernel, (meta.reshape(1, 112), hidden), sds((N_DP, 24, FEAT), BF))
    arrived = lax.all_to_all(outgoing, "dp", 0, 0, tiled=True)
    g1 = call(unpack_kernel, (row_counts, arrived.reshape(384, FEAT)), sds((128, FEAT), BF), in_specs=[SM, VM])
    digits = arrived[:, 16:24, 0:32].astype(F32)
    tokens = (digits[:, 0] + 256.0 * digits[:, 1] + 65536.0 * digits[:, 2]).astype(I32).reshape(1, 512)
    segments = digits[:, 3].astype(I32).reshape(1, 512)
    cots = (digits[:, 4] + digits[:, 5] + digits[:, 6]).reshape(1, 512)

    second = [g1] + [permute(g1, shift_perm("xy", 4 - d)) for d in (1, 2, 3)]
    hits, s = call(
        functools.partial(code_kernel, cols),
        (tokens, segments),
        [sds((512, cols), BF), sds((512, cols), F32)],
        cost=cost(1 << 20, 1 << 10),
    )
    second, s = lax.optimization_barrier((second, s))
    g2 = call(place_kernel, second, sds((4, 128, FEAT), BF))
    third = [g2] + [permute(g2, shift_perm("yx", 4 - d)) for d in (1, 2, 3)]

    wide = sds((512, cols), F32)
    small = cost(1 << 20, 1 << 10)
    quarter = sds((4, 128, FEAT), BF)
    pairs = ((1, 3), (2, 0))
    target_send, target_keep = call(
        target_products_kernel, (hits, head), [sds((4, 4, 128, FEAT), BF)] * 2, cost=small
    )
    other = permute(g2, CORE_PERM)
    s = call(first_scores_kernel, (g2, other, head, s), wide, cost=small, aliases={3: 0})
    *third, s, target_keep = lax.optimization_barrier((*third[1:], s, target_keep))
    other = [permute(v, CORE_PERM) for v in third]
    s = call(own_scores_kernel, (*third, head, s), wide, cost=small, aliases={4: 0})
    _, exps, stats = call(
        last_scores_kernel,
        (*other, head, s, hits),
        [wide, sds((512, cols), BF), sds((N_VOC, 16, 128), F32)],
        scratch=[pltpu.VMEM((512, 128), F32)],
        aliases={4: 0},
    )
    stats = lax.all_to_all(stats, "vocab", 0, 0, tiled=True)
    stats, chip = call(merge_kernel, (stats,), [sds((N_DP, 16, 128), F32), sds((8, 128), F32)])
    exps, chip, target_send = lax.optimization_barrier((exps, chip, target_send))
    target_got = permute(target_send, CORE_PERM)
    stats = lax.all_to_all(stats, "dp", 0, 0, tiled=True)
    got = {}
    for ds in pairs:
        out = call(functools.partial(send_products_kernel, ds), (exps, head), [quarter] * 2, cost=small)
        for d, v in zip(ds, out):
            got[d] = permute(v, CORE_PERM)
    factors, logprobs = call(
        factor_kernel, (stats, chip), [sds((512, 128), F32), sds((1, 32), F32)], scratch=[pltpu.VMEM((8, 128), F32)],
    )
    ring = {}
    for ds in pairs:
        out = call(
            functools.partial(combine_kernel, ds),
            (exps, head, factors, target_keep, target_got, *[got[d] for d in ds]),
            [quarter if d else sds((4, 128, FEAT), F32) for d in ds],
            cost=small,
        )
        for d, v in zip(ds, out):
            ring[d] = permute(v, shift_perm("yx", d)) if d else v
        factors, _ = lax.optimization_barrier((factors, out[0]))
    own, *out = call(ring_sum_kernel, [ring[d] for d in range(4)], [sds((128, FEAT), F32)] * 4)
    ring = [own] + [permute(v, shift_perm("xy", d + 1)) for d, v in enumerate(out)]
    back, slot, weight = call(
        ways_kernel,
        (row_counts, cots),
        [sds((256, 128), BF), sds((64, 256), BF), sds((64, 128), F32)],
        in_specs=[SM, VM],
        cost=small,
    )
    returning = call(return_kernel, (back, *ring), sds((256, FEAT), BF))
    returned = lax.all_to_all(returning.reshape(N_DP, 16, FEAT), "dp", 0, 0, tiled=True)
    grad_hidden = call(slots_kernel, (slot, weight, returned.reshape(256, FEAT)), sds((64, FEAT), BF))
    return logprobs.reshape(32), grad_hidden


def solution(mesh):
    return jax.shard_map(
        per_device,
        mesh=mesh,
        in_specs=(P("dp", "vocab"), P(None, ("dp", "vocab")), P(), P("dp"), P("dp"), P("dp")),
        out_specs=(P("dp"), P("dp", "vocab")),
        check_vma=False,
    )
```

```python
import functools

import jax
import jax.numpy as jnp
from jax import lax
from jax.experimental import pallas as pl
from jax.experimental.pallas import tpu as pltpu
from jax.sharding import PartitionSpec as P

freq_weight = 0.4
presence_weight = 0.8

N_DP, N_VOC = 16, 8
FEAT = 512
BF, F32, I32 = jnp.bfloat16, jnp.float32, jnp.int32
MIB = 1 << 20


def params(limit=32):
    return pltpu.CompilerParams(vmem_limit_bytes=limit * MIB)


def coords():
    dp, voc = lax.axis_index("dp"), lax.axis_index("vocab")
    return dp // 4, lax.rem(dp, 4), voc // 2, lax.rem(voc, 2)


def flat(x, z, y, c):
    return x * 32 + z * 8 + y * 2 + c


def shift_perm(axes, k):
    pairs = []
    for x in range(4):
        for z in range(4):
            for y in range(4):
                for c in range(2):
                    to = dict(x=x, z=z, y=y, c=c)
                    to[axes[c]] = (to[axes[c]] + k) % 4
                    pairs.append((flat(x, z, y, c), flat(**to)))
    return pairs


def pairing(axis, bits, cores=(0, 1)):
    pairs = []
    for x in range(4):
        for z in range(4):
            for y in range(4):
                for c in cores:
                    to = dict(x=x, z=z, y=y, c=c)
                    to[axis] ^= bits
                    pairs.append((flat(x, z, y, c), flat(**to)))
    return pairs


CORE_PERM = [(i, i ^ 1) for i in range(N_DP * N_VOC)]


def permute(v, pairs):
    return lax.ppermute(v, ("dp", "vocab"), pairs)


def iota(shape, dim):
    return lax.broadcasted_iota(I32, shape, dim)


VM = pl.BlockSpec(memory_space=pltpu.VMEM)


def my_slots(meta_ref):
    dp = lax.axis_index("dp")
    counts, lane = meta_ref[:, 0:16], iota((1, 16), 1)
    start = jnp.sum(jnp.where(lane < dp, counts, 0.0), axis=1, keepdims=True)
    count = jnp.sum(jnp.where(lane == dp, counts, 0.0), axis=1, keepdims=True)
    return start.astype(I32), count.astype(I32)


def pack_kernel(meta_ref, hid_ref, out_ref):
    start, count = my_slots(meta_ref)
    row, col = iota((64, 64), 0), iota((64, 64), 1)
    target = (row >> 4) * 4 + (row & 3)
    src = ((row >> 2) & 3) * N_DP + ((target - start) & 15)
    sel = (col == src) & (col < count)
    rows = jnp.dot(sel.astype(F32).astype(BF), hid_ref[...], preferred_element_type=F32).astype(BF)
    kind = iota((8, 32), 0)
    tok = meta_ref[:, 16:48].astype(I32)
    cot = meta_ref[:, 80:112]
    digit = jnp.where(kind == 0, tok & 255, jnp.where(kind == 1, (tok >> 8) & 255, tok >> 16)).astype(F32)
    digit = jnp.where(kind == 3, meta_ref[:, 48:80], digit)
    high = cot.astype(BF).astype(F32)
    mid = (cot - high).astype(BF).astype(F32)
    low = cot - high - mid
    digit = jnp.where(kind < 4, digit, jnp.where(kind == 4, high, jnp.where(kind == 5, mid, low))).astype(BF)
    for a in range(N_DP):
        out_ref[a, 0:16, :] = rows[(a // 4) * 16:(a // 4) * 16 + 16]
        out_ref[a, 16:24, :] = jnp.zeros((8, FEAT), BF)
        out_ref[a, 16:24, 0:32] = digit


def placing(meta_ref, shape, slot_dim, per_source):
    x = lax.axis_index("dp") // 4
    line = (shape[0], 1) if slot_dim == 0 else (1, shape[1])
    k, row = iota(line, slot_dim), iota(shape, 1 - slot_dim)
    s = k >> 4 if per_source == 16 else (k * 2731) >> 16
    u = k - s * per_source
    t, z = u >> 2, u & 3
    start = jnp.zeros(line, F32)
    count = jnp.zeros(line, F32)
    for i in range(N_DP):
        live = meta_ref[:, i:i + 1]
        start = start + jnp.where(s > i, live, 0.0)
        count = jnp.where(s == i, live, count)
    start, count = start.astype(I32), count.astype(I32)
    a = x * 4 + z
    offset = (a - start) & 15
    base = (start + offset - a) >> 4
    at = jnp.where((u < 16) & (t * N_DP + offset < count), z * 32 + base + t, -1)
    return (at == row).astype(F32).astype(BF)


def unpack_kernel(meta_ref, arr_ref, out_ref):
    sel = placing(meta_ref, (128, 384), 1, 24)
    out_ref[...] = jnp.dot(sel, arr_ref[...], preferred_element_type=F32).astype(BF)


def place_kernel(a0, a1, a2, a3, out_ref):
    x, z, y, c = coords()
    own = jnp.where(c == 0, x, y)
    for d, a in enumerate((a0, a1, a2, a3)):
        out_ref[pl.ds((own + d) & 3, 1)] = a[...][None]


def column(row):
    wide = jnp.broadcast_to(row, (128, row.shape[1]))
    return jnp.transpose(wide)[:, 0:1]


def code_kernel(cols, tok_ref, seg_ref, hit_ref, start_ref):
    dp, voc = lax.axis_index("dp"), lax.axis_index("vocab")
    tok, seg = tok_ref[...], seg_ref[...]
    tok_col = column(tok.astype(F32)).astype(I32)
    seg_col = column(seg.astype(F32)).astype(I32)
    prior = (seg_col == seg) & (iota((512, 512), 1) < iota((512, 512), 0))
    prior = prior.astype(F32).astype(BF)
    first = (dp * N_VOC + voc) * cols
    hits = (tok_col == first + iota((512, cols), 1)).astype(F32).astype(BF)
    hit_ref[...] = hits
    counts = jnp.dot(prior, hits, preferred_element_type=F32)
    start_ref[...] = -(freq_weight * counts) - presence_weight * (counts > 0).astype(F32)


def features(yy, core):
    return pl.ds(pl.multiple_of((yy * 2 + core) * FEAT, FEAT), FEAT)


def block_scores(ds, zero, one, head_ref, s_in, s_ref):
    x, z, y, c = coords()
    dims = (((1,), (1,)), ((), ()))
    if zero is not None:
        part = s_in[...]
        for d, block in zip(ds, zero):
            w = head_ref[:, features((y + d) & 3, 0)]
            part += lax.dot_general(block[...].reshape(512, FEAT), w, dims, preferred_element_type=F32)
        s_ref[...] = part
    else:
        s_ref[...] = s_in[...]
    if one is not None:
        def step(q, _):
            rows = jnp.concatenate([block[q] for block in one], axis=0)
            part = lax.dot_general(rows, head_ref[:, features(q, 1)], dims, preferred_element_type=F32)
            for i, d in enumerate(ds):
                s_ref[pl.ds(pl.multiple_of(((x + d) & 3) * 128, 128), 128), :] += part[i * 128:(i + 1) * 128]
            return _

        lax.fori_loop(0, 4, step, 0)


def both_scores(ds, own, other, head_ref, s_in, s_ref):
    c = coords()[3]

    @pl.when(c == 0)
    def _():
        block_scores(ds, own, other, head_ref, s_in, s_ref)

    @pl.when(c == 1)
    def _():
        block_scores(ds, other, own, head_ref, s_in, s_ref)


def first_scores_kernel(own, other, head_ref, s_in, s_ref):
    both_scores((0,), (own,), (other,), head_ref, s_in, s_ref)


def own_scores_kernel(a1, a2, a3, head_ref, s_in, s_ref):
    both_scores((1, 2, 3), (a1, a2, a3), None, head_ref, s_in, s_ref)


def last_scores_kernel(a1, a2, a3, head_ref, s_in, hit_ref, s_ref, exp_ref, stat_ref, ss):
    both_scores((1, 2, 3), None, (a1, a2, a3), head_ref, s_in, s_ref)

    def rows(i, _):
        at = pl.ds(pl.multiple_of(i * 32, 32), 32)
        s = s_ref[at, :]
        hit = hit_ref[at, :].astype(F32) > 0.5
        m = jnp.max(s, axis=1, keepdims=True)
        e = jnp.exp(s - m)
        exp_ref[at, :] = jnp.where(hit, 0.0, e).astype(BF)
        ss[at, 0:1] = m
        ss[at, 1:2] = jnp.sum(e, axis=1, keepdims=True)
        ss[at, 2:3] = jnp.sum(jnp.where(hit, s, 0.0), axis=1, keepdims=True)
        return _

    lax.fori_loop(0, 16, rows, 0, unroll=4)
    flat_stats = jnp.transpose(ss[...])
    for j in range(3):
        for k in range(4):
            stat_ref[j * 4 + k:j * 4 + k + 1, :] = flat_stats[j:j + 1, k * 128:(k + 1) * 128]
    stat_ref[12:16, :] = jnp.zeros((4, 128), F32)


def merge(found):
    m = functools.reduce(jnp.maximum, [st[0:4, :] for st in found])
    total = sum(st[4:8, :] * jnp.exp(st[0:4, :] - m) for st in found)
    return m, total, sum(st[8:12, :] for st in found)


def chip_kernel(a_ref, b_ref, out_ref, chip_ref):
    out_ref[0:4, :], out_ref[4:8, :], out_ref[8:12, :] = merge((a_ref, b_ref))
    out_ref[12:16, :] = jnp.zeros((4, 128), F32)
    chip_ref[0:4, :] = a_ref[0:4, :]
    chip_ref[4:8, :] = b_ref[0:4, :]


def line_kernel(s0, s1, s2, s3, out_ref):
    m, total, picked = merge((s0, s1, s2, s3))
    for n in range(N_DP):
        out_ref[n, 0:4, :] = m
        out_ref[n, 4:8, :] = total
        out_ref[n, 8:12, :] = picked
        out_ref[n, 12:16, :] = jnp.zeros((4, 128), F32)


def long_row(v):
    return jnp.concatenate([v[k:k + 1, :] for k in range(4)], axis=1)


def columns(rows, out_ref):
    place = iota((128, rows[0].shape[1]), 0)
    wide = jnp.zeros(place.shape, F32)
    for i, row in enumerate(rows):
        wide = jnp.where(place == i, row, wide)
    out_ref[...] = jnp.transpose(wide)


def factor_kernel(st_ref, chip_ref, factor_ref, lp_ref, lps):
    x, z, y, c = coords()
    m, total, picked = merge([st_ref.at[n] for n in range(N_DP)])
    lps[0:4, :] = picked - m - jnp.log(total)
    mine = pltpu.roll(lps[pl.ds(x, 1), :], (128 - 32 * z) & 127, 1)
    lp_ref[...] = mine[:, 0:32]
    own, other = (jnp.exp(chip_ref[i:i + 4, :] - m) / total for i in (0, 4))
    columns([long_row(v) for v in (own, other, 1.0 - jnp.exp(picked - m) / total)], factor_ref)


def block_products(ds, core, left_ref, head_ref, put):
    x, z, y, c = coords()

    @pl.when(core == 0)
    def _():
        def one(i, d):
            v = jnp.dot(left_ref[...], head_ref[:, features((y + d) & 3, 0)], preferred_element_type=F32)
            for q in range(4):
                put(i, q, q * 128, v[q * 128:(q + 1) * 128])

        if ds == (0, 1, 2, 3):
            lax.fori_loop(0, 4, lambda d, _: one(d, d) or _, 0)
        else:
            for i, d in enumerate(ds):
                one(i, d)

    @pl.when(core == 1)
    def _():
        def step(q, _):
            ats = [pl.multiple_of(((x + d) & 3) * 128, 128) for d in ds]
            rows = jnp.concatenate([left_ref[pl.ds(at, 128), :] for at in ats], axis=0)
            v = jnp.dot(rows, head_ref[:, features(q, 1)], preferred_element_type=F32)
            for i, at in enumerate(ats):
                put(i, q, at, v[i * 128:(i + 1) * 128])
            return _

        lax.fori_loop(0, 4, step, 0)


def send_products_kernel(ds, left_ref, head_ref, *outs):
    def put(i, q, at, v):
        outs[i][q] = v.astype(BF)

    block_products(ds, 1 - coords()[3], left_ref, head_ref, put)


def target_products_kernel(left_ref, head_ref, send_ref, keep_ref):
    c = coords()[3]
    for core, out in ((1 - c, send_ref), (c, keep_ref)):
        def put(i, q, at, v, out=out):
            out[i, q] = v.astype(BF)

        block_products((0, 1, 2, 3), core, left_ref, head_ref, put)


def combine_kernel(ds, left_ref, head_ref, factor_ref, tk_ref, tg_ref, *refs):
    got, outs = refs[:len(ds)], refs[len(ds):]

    def put(i, q, at, v):
        f = factor_ref[pl.ds(at, 128), :]
        target = tk_ref[ds[i], q].astype(F32) + tg_ref[ds[i], q].astype(F32)
        v = target * f[:, 2:3] - (v * f[:, 0:1] + got[i][q].astype(F32) * f[:, 1:2])
        outs[i][q] = v.astype(outs[i].dtype)

    block_products(ds, coords()[3], left_ref, head_ref, put)


def ring_sum_kernel(own_in, r1, r2, r3, own_ref, b1, b2, b3):
    x, z, y, c = coords()
    own = jnp.where(c == 0, x, y)
    for d, out in enumerate((own_ref, b1, b2, b3)):
        q = (own + d) & 3
        out[...] = own_in[q] + r1[q].astype(F32) + r2[q].astype(F32) + r3[q].astype(F32)


def ways_kernel(meta_ref, cot_ref, back_ref, slot_ref, weight_ref):
    back_ref[...] = placing(meta_ref, (256, 128), 0, 16)
    start, count = my_slots(meta_ref)
    j, k = iota((64, 256), 0), iota((64, 256), 1)
    a = (start + j) & 15
    sel = ((k >> 6) == (a >> 2)) & (((k >> 2) & 3) == (j >> 4)) & ((k & 3) == (a & 3)) & (j < count)
    slot_ref[...] = sel.astype(F32).astype(BF)
    g = start + iota((64, 512), 0)
    here = iota((64, 512), 1) == (g & 15) * 32 + (g >> 4)
    cot = jnp.sum(jnp.where(here, cot_ref[...], 0.0), axis=1, keepdims=True)
    weight_ref[...] = jnp.broadcast_to(cot, (64, 128))


def return_kernel(back_ref, own_in, r1, r2, r3, out_ref):
    v = (own_in[...] + r1[...] + r2[...] + r3[...]).astype(BF)
    out_ref[...] = jnp.dot(back_ref[...], v, preferred_element_type=F32).astype(BF)


def slots_kernel(slot_ref, weight_ref, arr_ref, out_ref):
    v = jnp.dot(slot_ref[...], arr_ref[...], preferred_element_type=F32)
    out_ref[...] = (v * weight_ref[:, 0:1]).astype(BF)


def sds(shape, dtype):
    return jax.ShapeDtypeStruct(shape, dtype)


def call(kernel, ins, outs, in_specs=None, scratch=(), limit=12, cost=None, aliases=None):
    multi = isinstance(outs, (list, tuple))
    return pl.pallas_call(
        kernel,
        out_shape=outs,
        in_specs=in_specs or [VM] * len(ins),
        out_specs=[VM] * len(outs) if multi else VM,
        scratch_shapes=list(scratch),
        compiler_params=params(limit),
        cost_estimate=cost,
        input_output_aliases=aliases or {},
    )(*ins)


def cost(flops, nbytes):
    return pl.CostEstimate(flops=flops, bytes_accessed=nbytes, transcendentals=0)


def per_device(hidden, head, row_counts, token_ids, segment_ids, cotangent):
    cols = head.shape[1]
    head = head.T
    meta = jnp.pad(row_counts, (0, 96)) + jnp.pad(token_ids, (16, 64)) + jnp.pad(segment_ids, (48, 32))
    meta = meta.astype(F32) + jnp.pad(cotangent, (80, 0))
    meta = meta.reshape(1, 112)
    outgoing = call(pack_kernel, (meta, hidden), sds((N_DP, 24, FEAT), BF))
    arrived = lax.all_to_all(outgoing, "dp", 0, 0, tiled=True)
    g1 = call(unpack_kernel, (meta, arrived.reshape(384, FEAT)), sds((128, FEAT), BF))
    digits = arrived[:, 16:24, 0:32].astype(F32)
    tokens = (digits[:, 0] + 256.0 * digits[:, 1] + 65536.0 * digits[:, 2]).astype(I32).reshape(1, 512)
    segments = digits[:, 3].astype(I32).reshape(1, 512)
    cots = (digits[:, 4] + digits[:, 5] + digits[:, 6]).reshape(1, 512)

    second = [g1] + [permute(g1, shift_perm("xy", 4 - d)) for d in (1, 2, 3)]
    hits, s = call(
        functools.partial(code_kernel, cols),
        (tokens, segments),
        [sds((512, cols), BF), sds((512, cols), F32)],
        cost=cost(1 << 20, 1 << 10),
    )
    second, s = lax.optimization_barrier((second, s))
    g2 = call(place_kernel, second, sds((4, 128, FEAT), BF))
    third = [g2] + [permute(g2, shift_perm("yx", 4 - d)) for d in (1, 2, 3)]

    wide = sds((512, cols), F32)
    small = cost(1 << 20, 1 << 10)
    quarter = sds((4, 128, FEAT), BF)
    pairs = ((1, 3), (2, 0))
    target_send, target_keep = call(
        target_products_kernel, (hits, head), [sds((4, 4, 128, FEAT), BF)] * 2, cost=small
    )
    other = permute(g2, CORE_PERM)
    s = call(first_scores_kernel, (g2, other, head, s), wide, cost=small, aliases={3: 0})
    *third, s, target_keep = lax.optimization_barrier((*third[1:], s, target_keep))
    other = [permute(v, CORE_PERM) for v in third]
    s = call(own_scores_kernel, (*third, head, s), wide, cost=small, aliases={4: 0})
    _, exps, stats = call(
        last_scores_kernel,
        (*other, head, s, hits),
        [wide, sds((512, cols), BF), sds((16, 128), F32)],
        scratch=[pltpu.VMEM((512, 128), F32)],
        aliases={4: 0},
    )
    stats, chip = call(
        chip_kernel, (stats, permute(stats, CORE_PERM)), [sds((16, 128), F32), sds((8, 128), F32)]
    )
    line = [stats] + [permute(stats, shift_perm("yy", d)) for d in (1, 2, 3)]
    send = {}
    for ds in pairs:
        out = call(functools.partial(send_products_kernel, ds), (exps, head), [quarter] * 2, cost=small)
        send.update(zip(ds, out))
    line, send, target_send = lax.optimization_barrier((line, send, target_send))
    stats = call(line_kernel, line, sds((N_DP, 16, 128), F32))
    got = {d: permute(send[d], CORE_PERM) for d in (1, 3, 2, 0)}
    target_got = permute(target_send, CORE_PERM)
    stats = lax.all_to_all(stats, "dp", 0, 0, tiled=True)
    factors, logprobs = call(
        factor_kernel, (stats, chip), [sds((512, 128), F32), sds((1, 32), F32)], scratch=[pltpu.VMEM((8, 128), F32)],
    )
    ring = {}
    for ds in pairs:
        out = call(
            functools.partial(combine_kernel, ds),
            (exps, head, factors, target_keep, target_got, *[got[d] for d in ds]),
            [quarter if d else sds((4, 128, FEAT), F32) for d in ds],
            cost=cost(3 << 30, 1 << 10),
        )
        for d, v in zip(ds, out):
            ring[d] = permute(v, shift_perm("yx", d)) if d else v
        factors, _ = lax.optimization_barrier((factors, out[0]))
    own, *out = call(ring_sum_kernel, [ring[d] for d in range(4)], [sds((128, FEAT), F32)] * 4)
    ring = [own] + [permute(v, shift_perm("xy", d + 1)) for d, v in enumerate(out)]
    back, slot, weight = call(
        ways_kernel,
        (meta, cots),
        [sds((256, 128), BF), sds((64, 256), BF), sds((64, 128), F32)],
        cost=small,
    )
    returning = call(return_kernel, (back, *ring), sds((256, FEAT), BF))
    returned = lax.all_to_all(returning.reshape(N_DP, 16, FEAT), "dp", 0, 0, tiled=True)
    grad_hidden = call(slots_kernel, (slot, weight, returned.reshape(256, FEAT)), sds((64, FEAT), BF))
    return logprobs.reshape(32), grad_hidden


def solution(mesh):
    return jax.shard_map(
        per_device,
        mesh=mesh,
        in_specs=(P("dp", "vocab"), P(None, ("dp", "vocab")), P(), P("dp"), P("dp"), P("dp")),
        out_specs=(P("dp"), P("dp", "vocab")),
        check_vma=False,
    )
```

```python
import functools

import jax
import jax.numpy as jnp
from jax import lax
from jax.experimental import pallas as pl
from jax.experimental.pallas import tpu as pltpu
from jax.sharding import PartitionSpec as P

freq_weight = 0.4
presence_weight = 0.8

N_DP, N_VOC = 16, 8
FEAT = 512
BF, F32, I32 = jnp.bfloat16, jnp.float32, jnp.int32
MIB = 1 << 20


def params(limit=32):
    return pltpu.CompilerParams(vmem_limit_bytes=limit * MIB)


def coords():
    dp, voc = lax.axis_index("dp"), lax.axis_index("vocab")
    return dp // 4, lax.rem(dp, 4), voc // 2, lax.rem(voc, 2)


def flat(x, z, y, c):
    return x * 32 + z * 8 + y * 2 + c


def shift_perm(axes, k):
    pairs = []
    for x in range(4):
        for z in range(4):
            for y in range(4):
                for c in range(2):
                    to = dict(x=x, z=z, y=y, c=c)
                    to[axes[c]] = (to[axes[c]] + k) % 4
                    pairs.append((flat(x, z, y, c), flat(**to)))
    return pairs


def pairing(axis, bits, cores=(0, 1)):
    pairs = []
    for x in range(4):
        for z in range(4):
            for y in range(4):
                for c in cores:
                    to = dict(x=x, z=z, y=y, c=c)
                    to[axis] ^= bits
                    pairs.append((flat(x, z, y, c), flat(**to)))
    return pairs


CORE_PERM = [(i, i ^ 1) for i in range(N_DP * N_VOC)]


def permute(v, pairs):
    return lax.ppermute(v, ("dp", "vocab"), pairs)


def iota(shape, dim):
    return lax.broadcasted_iota(I32, shape, dim)


VM = pl.BlockSpec(memory_space=pltpu.VMEM)


def my_slots(meta_ref):
    dp = lax.axis_index("dp")
    counts, lane = meta_ref[:, 0:16], iota((1, 16), 1)
    start = jnp.sum(jnp.where(lane < dp, counts, 0.0), axis=1, keepdims=True)
    count = jnp.sum(jnp.where(lane == dp, counts, 0.0), axis=1, keepdims=True)
    return start.astype(I32), count.astype(I32)


def pack_kernel(meta_ref, hid_ref, out_ref):
    start, count = my_slots(meta_ref)
    row, col = iota((64, 64), 0), iota((64, 64), 1)
    target = (row >> 4) * 4 + (row & 3)
    src = ((row >> 2) & 3) * N_DP + ((target - start) & 15)
    sel = (col == src) & (col < count)
    rows = jnp.dot(sel.astype(F32).astype(BF), hid_ref[...], preferred_element_type=F32).astype(BF)
    kind = iota((8, 32), 0)
    tok = meta_ref[:, 16:48].astype(I32)
    cot = meta_ref[:, 80:112]
    digit = jnp.where(kind == 0, tok & 255, jnp.where(kind == 1, (tok >> 8) & 255, tok >> 16)).astype(F32)
    digit = jnp.where(kind == 3, meta_ref[:, 48:80], digit)
    high = cot.astype(BF).astype(F32)
    mid = (cot - high).astype(BF).astype(F32)
    low = cot - high - mid
    digit = jnp.where(kind < 4, digit, jnp.where(kind == 4, high, jnp.where(kind == 5, mid, low))).astype(BF)
    for a in range(N_DP):
        out_ref[a, 0:16, :] = rows[(a // 4) * 16:(a // 4) * 16 + 16]
        out_ref[a, 16:24, :] = jnp.zeros((8, FEAT), BF)
        out_ref[a, 16:24, 0:32] = digit


def placing(meta_ref, shape, slot_dim, per_source):
    x = lax.axis_index("dp") // 4
    line = (shape[0], 1) if slot_dim == 0 else (1, shape[1])
    k, row = iota(line, slot_dim), iota(shape, 1 - slot_dim)
    s = k >> 4 if per_source == 16 else (k * 2731) >> 16
    u = k - s * per_source
    t, z = u >> 2, u & 3
    start = jnp.zeros(line, F32)
    count = jnp.zeros(line, F32)
    for i in range(N_DP):
        live = meta_ref[:, i:i + 1]
        start = start + jnp.where(s > i, live, 0.0)
        count = jnp.where(s == i, live, count)
    start, count = start.astype(I32), count.astype(I32)
    a = x * 4 + z
    offset = (a - start) & 15
    base = (start + offset - a) >> 4
    at = jnp.where((u < 16) & (t * N_DP + offset < count), z * 32 + base + t, -1)
    return (at == row).astype(F32).astype(BF)


def unpack_kernel(meta_ref, arr_ref, out_ref):
    sel = placing(meta_ref, (128, 384), 1, 24)
    out_ref[...] = jnp.dot(sel, arr_ref[...], preferred_element_type=F32).astype(BF)


def place_kernel(a0, a1, a2, a3, out_ref):
    x, z, y, c = coords()
    own = jnp.where(c == 0, x, y)
    for d, a in enumerate((a0, a1, a2, a3)):
        out_ref[pl.ds((own + d) & 3, 1)] = a[...][None]


def column(row):
    wide = jnp.broadcast_to(row, (128, row.shape[1]))
    return jnp.transpose(wide)[:, 0:1]


def code_kernel(cols, tok_ref, seg_ref, hit_ref, start_ref):
    dp, voc = lax.axis_index("dp"), lax.axis_index("vocab")
    tok, seg = tok_ref[...], seg_ref[...]
    tok_col = column(tok.astype(F32)).astype(I32)
    seg_col = column(seg.astype(F32)).astype(I32)
    prior = (seg_col == seg) & (iota((512, 512), 1) < iota((512, 512), 0))
    prior = prior.astype(F32).astype(BF)
    first = (dp * N_VOC + voc) * cols
    hits = (tok_col == first + iota((512, cols), 1)).astype(F32).astype(BF)
    hit_ref[...] = hits
    counts = jnp.dot(prior, hits, preferred_element_type=F32)
    start_ref[...] = -(freq_weight * counts) - presence_weight * (counts > 0).astype(F32)


def features(yy, core):
    return pl.ds(pl.multiple_of((yy * 2 + core) * FEAT, FEAT), FEAT)


def block_scores(ds, zero, one, head_ref, s_in, s_ref):
    x, z, y, c = coords()
    dims = (((1,), (1,)), ((), ()))
    if zero is not None:
        part = s_in[...]
        for d, block in zip(ds, zero):
            w = head_ref[:, features((y + d) & 3, 0)]
            part += lax.dot_general(block[...].reshape(512, FEAT), w, dims, preferred_element_type=F32)
        s_ref[...] = part
    else:
        s_ref[...] = s_in[...]
    if one is not None:
        def step(q, _):
            rows = jnp.concatenate([block[q] for block in one], axis=0)
            part = lax.dot_general(rows, head_ref[:, features(q, 1)], dims, preferred_element_type=F32)
            for i, d in enumerate(ds):
                s_ref[pl.ds(pl.multiple_of(((x + d) & 3) * 128, 128), 128), :] += part[i * 128:(i + 1) * 128]
            return _

        lax.fori_loop(0, 4, step, 0)


def both_scores(ds, own, other, head_ref, s_in, s_ref):
    c = coords()[3]

    @pl.when(c == 0)
    def _():
        block_scores(ds, own, other, head_ref, s_in, s_ref)

    @pl.when(c == 1)
    def _():
        block_scores(ds, other, own, head_ref, s_in, s_ref)


def first_scores_kernel(own, other, head_ref, s_in, s_ref):
    both_scores((0,), (own,), (other,), head_ref, s_in, s_ref)


def own_scores_kernel(a1, a2, a3, head_ref, s_in, s_ref):
    both_scores((1, 2, 3), (a1, a2, a3), None, head_ref, s_in, s_ref)


def last_scores_kernel(a1, a2, a3, head_ref, s_in, hit_ref, s_ref, exp_ref, stat_ref, ss):
    both_scores((1, 2, 3), None, (a1, a2, a3), head_ref, s_in, s_ref)

    def rows(i, _):
        at = pl.ds(pl.multiple_of(i * 32, 32), 32)
        s = s_ref[at, :]
        hit = hit_ref[at, :].astype(F32) > 0.5
        m = jnp.max(s, axis=1, keepdims=True)
        e = jnp.exp(s - m)
        exp_ref[at, :] = jnp.where(hit, 0.0, e).astype(BF)
        ss[at, 0:1] = m
        ss[at, 1:2] = jnp.sum(e, axis=1, keepdims=True)
        ss[at, 2:3] = jnp.sum(jnp.where(hit, s, 0.0), axis=1, keepdims=True)
        return _

    lax.fori_loop(0, 16, rows, 0, unroll=4)
    flat_stats = jnp.transpose(ss[...])
    for j in range(3):
        for k in range(4):
            stat_ref[j * 4 + k:j * 4 + k + 1, :] = flat_stats[j:j + 1, k * 128:(k + 1) * 128]
    stat_ref[12:16, :] = jnp.zeros((4, 128), F32)


def merge(found):
    m = functools.reduce(jnp.maximum, [st[0:4, :] for st in found])
    total = sum(st[4:8, :] * jnp.exp(st[0:4, :] - m) for st in found)
    return m, total, sum(st[8:12, :] for st in found)


def chip_kernel(a_ref, b_ref, out_ref, chip_ref):
    out_ref[0:4, :], out_ref[4:8, :], out_ref[8:12, :] = merge((a_ref, b_ref))
    out_ref[12:16, :] = jnp.zeros((4, 128), F32)
    chip_ref[0:4, :] = a_ref[0:4, :]
    chip_ref[4:8, :] = b_ref[0:4, :]


def line_kernel(s0, s1, s2, s3, out_ref):
    m, total, picked = merge((s0, s1, s2, s3))
    for n in range(N_DP):
        out_ref[n, 0:4, :] = m
        out_ref[n, 4:8, :] = total
        out_ref[n, 8:12, :] = picked
        out_ref[n, 12:16, :] = jnp.zeros((4, 128), F32)


def long_row(v):
    return jnp.concatenate([v[k:k + 1, :] for k in range(4)], axis=1)


def columns(rows, out_ref):
    place = iota((128, rows[0].shape[1]), 0)
    wide = jnp.zeros(place.shape, F32)
    for i, row in enumerate(rows):
        wide = jnp.where(place == i, row, wide)
    out_ref[...] = jnp.transpose(wide)


def factor_kernel(st_ref, chip_ref, factor_ref, lp_ref, lps):
    x, z, y, c = coords()
    m, total, picked = merge([st_ref.at[n] for n in range(N_DP)])
    lps[0:4, :] = picked - m - jnp.log(total)
    mine = pltpu.roll(lps[pl.ds(x, 1), :], (128 - 32 * z) & 127, 1)
    lp_ref[...] = mine[:, 0:32]
    own, other = (jnp.exp(chip_ref[i:i + 4, :] - m) / total for i in (0, 4))
    columns([long_row(v) for v in (own, other, 1.0 - jnp.exp(picked - m) / total)], factor_ref)


def block_products(ds, core, left_ref, head_ref, put):
    x, z, y, c = coords()

    @pl.when(core == 0)
    def _():
        def one(i, d):
            v = jnp.dot(left_ref[...], head_ref[:, features((y + d) & 3, 0)], preferred_element_type=F32)
            for q in range(4):
                put(i, q, q * 128, v[q * 128:(q + 1) * 128])

        if ds == (0, 1, 2, 3):
            lax.fori_loop(0, 4, lambda d, _: one(d, d) or _, 0)
        else:
            for i, d in enumerate(ds):
                one(i, d)

    @pl.when(core == 1)
    def _():
        def step(q, _):
            ats = [pl.multiple_of(((x + d) & 3) * 128, 128) for d in ds]
            rows = jnp.concatenate([left_ref[pl.ds(at, 128), :] for at in ats], axis=0)
            v = jnp.dot(rows, head_ref[:, features(q, 1)], preferred_element_type=F32)
            for i, at in enumerate(ats):
                put(i, q, at, v[i * 128:(i + 1) * 128])
            return _

        lax.fori_loop(0, 4, step, 0)


def send_products_kernel(ds, left_ref, head_ref, *outs):
    def put(i, q, at, v):
        outs[i][q] = v.astype(BF)

    block_products(ds, 1 - coords()[3], left_ref, head_ref, put)


def target_products_kernel(left_ref, head_ref, send_ref, keep_ref):
    c = coords()[3]
    for core, out in ((1 - c, send_ref), (c, keep_ref)):
        def put(i, q, at, v, out=out):
            out[i, q] = v.astype(BF)

        block_products((0, 1, 2, 3), core, left_ref, head_ref, put)


def combine_kernel(ds, left_ref, head_ref, factor_ref, tk_ref, tg_ref, *refs):
    got, outs = refs[:len(ds)], refs[len(ds):]

    def put(i, q, at, v):
        f = factor_ref[pl.ds(at, 128), :]
        target = tk_ref[ds[i], q].astype(F32) + tg_ref[ds[i], q].astype(F32)
        v = target * f[:, 2:3] - (v * f[:, 0:1] + got[i][q].astype(F32) * f[:, 1:2])
        outs[i][q] = v.astype(outs[i].dtype)

    block_products(ds, coords()[3], left_ref, head_ref, put)


def ring_sum_kernel(own_in, r1, r2, r3, own_ref, b1, b2, b3):
    x, z, y, c = coords()
    own = jnp.where(c == 0, x, y)
    for d, out in enumerate((own_ref, b1, b2, b3)):
        q = (own + d) & 3
        out[...] = own_in[q] + r1[q].astype(F32) + r2[q].astype(F32) + r3[q].astype(F32)


def ways_kernel(meta_ref, cot_ref, back_ref, slot_ref, weight_ref):
    back_ref[...] = placing(meta_ref, (256, 128), 0, 16)
    start, count = my_slots(meta_ref)
    j, k = iota((64, 256), 0), iota((64, 256), 1)
    a = (start + j) & 15
    sel = ((k >> 6) == (a >> 2)) & (((k >> 2) & 3) == (j >> 4)) & ((k & 3) == (a & 3)) & (j < count)
    slot_ref[...] = sel.astype(F32).astype(BF)
    g = start + iota((64, 512), 0)
    here = iota((64, 512), 1) == (g & 15) * 32 + (g >> 4)
    cot = jnp.sum(jnp.where(here, cot_ref[...], 0.0), axis=1, keepdims=True)
    weight_ref[...] = jnp.broadcast_to(cot, (64, 128))


def return_kernel(back_ref, own_in, r1, r2, r3, out_ref):
    v = (own_in[...] + r1[...] + r2[...] + r3[...]).astype(BF)
    out_ref[...] = jnp.dot(back_ref[...], v, preferred_element_type=F32).astype(BF)


def slots_kernel(slot_ref, weight_ref, arr_ref, out_ref):
    v = jnp.dot(slot_ref[...], arr_ref[...], preferred_element_type=F32)
    out_ref[...] = (v * weight_ref[:, 0:1]).astype(BF)


def sds(shape, dtype):
    return jax.ShapeDtypeStruct(shape, dtype)


def call(kernel, ins, outs, in_specs=None, scratch=(), limit=12, cost=None, aliases=None):
    multi = isinstance(outs, (list, tuple))
    return pl.pallas_call(
        kernel,
        out_shape=outs,
        in_specs=in_specs or [VM] * len(ins),
        out_specs=[VM] * len(outs) if multi else VM,
        scratch_shapes=list(scratch),
        compiler_params=params(limit),
        cost_estimate=cost,
        input_output_aliases=aliases or {},
    )(*ins)


def cost(flops, nbytes):
    return pl.CostEstimate(flops=flops, bytes_accessed=nbytes, transcendentals=0)


def per_device(hidden, head, row_counts, token_ids, segment_ids, cotangent):
    cols = head.shape[1]
    head = head.T
    meta = jnp.pad(row_counts, (0, 96)) + jnp.pad(token_ids, (16, 64)) + jnp.pad(segment_ids, (48, 32))
    meta = meta.astype(F32) + jnp.pad(cotangent, (80, 0))
    meta = meta.reshape(1, 112)
    outgoing = call(pack_kernel, (meta, hidden), sds((N_DP, 24, FEAT), BF))
    arrived = lax.all_to_all(outgoing, "dp", 0, 0, tiled=True)
    g1 = call(unpack_kernel, (meta, arrived.reshape(384, FEAT)), sds((128, FEAT), BF))
    digits = arrived[:, 16:24, 0:32].astype(F32)
    tokens = (digits[:, 0] + 256.0 * digits[:, 1] + 65536.0 * digits[:, 2]).astype(I32).reshape(1, 512)
    segments = digits[:, 3].astype(I32).reshape(1, 512)
    cots = (digits[:, 4] + digits[:, 5] + digits[:, 6]).reshape(1, 512)

    second = [g1] + [permute(g1, shift_perm("xy", 4 - d)) for d in (1, 2, 3)]
    hits, s = call(
        functools.partial(code_kernel, cols),
        (tokens, segments),
        [sds((512, cols), BF), sds((512, cols), F32)],
        cost=cost(1 << 20, 1 << 10),
    )
    second, s = lax.optimization_barrier((second, s))
    g2 = call(place_kernel, second, sds((4, 128, FEAT), BF))
    third = [g2] + [permute(g2, shift_perm("yx", 4 - d)) for d in (1, 2, 3)]

    wide = sds((512, cols), F32)
    small = cost(1 << 20, 1 << 10)
    quarter = sds((4, 128, FEAT), BF)
    pairs = ((1, 3), (2, 0))
    target_send, target_keep = call(
        target_products_kernel, (hits, head), [sds((4, 4, 128, FEAT), BF)] * 2, cost=small
    )
    other = permute(g2, CORE_PERM)
    s = call(first_scores_kernel, (g2, other, head, s), wide, cost=small, aliases={3: 0})
    *third, s, target_keep = lax.optimization_barrier((*third[1:], s, target_keep))
    other = [permute(v, CORE_PERM) for v in third]
    s = call(own_scores_kernel, (*third, head, s), wide, cost=small, aliases={4: 0})
    _, exps, stats = call(
        last_scores_kernel,
        (*other, head, s, hits),
        [wide, sds((512, cols), BF), sds((16, 128), F32)],
        scratch=[pltpu.VMEM((512, 128), F32)],
        aliases={4: 0},
    )
    stats, chip = call(
        chip_kernel, (stats, permute(stats, CORE_PERM)), [sds((16, 128), F32), sds((8, 128), F32)]
    )
    line = [stats] + [permute(stats, shift_perm("yy", d)) for d in (1, 2, 3)]
    send = {}
    for ds in pairs:
        out = call(functools.partial(send_products_kernel, ds), (exps, head), [quarter] * 2, cost=small)
        send.update(zip(ds, out))
    line, send, target_send = lax.optimization_barrier((line, send, target_send))
    stats = call(line_kernel, line, sds((N_DP, 16, 128), F32))
    got = {d: permute(send[d], CORE_PERM) for d in (2, 1, 3, 0)}
    target_got = permute(target_send, CORE_PERM)
    stats = lax.all_to_all(stats, "dp", 0, 0, tiled=True)
    factors, logprobs = call(
        factor_kernel, (stats, chip), [sds((512, 128), F32), sds((1, 32), F32)], scratch=[pltpu.VMEM((8, 128), F32)],
    )
    ring = {}
    for ds in ((2, 1), (3, 0)):
        out = call(
            functools.partial(combine_kernel, ds),
            (exps, head, factors, target_keep, target_got, *[got[d] for d in ds]),
            [quarter if d else sds((4, 128, FEAT), F32) for d in ds],
            cost=cost(3 << 30, 1 << 10),
        )
        for d, v in zip(ds, out):
            ring[d] = permute(v, shift_perm("yx", d)) if d else v
        factors, _ = lax.optimization_barrier((factors, out[0]))
    own, *out = call(ring_sum_kernel, [ring[d] for d in range(4)], [sds((128, FEAT), F32)] * 4)
    ring = [own] + [permute(v, shift_perm("xy", d + 1)) for d, v in enumerate(out)]
    back, slot, weight = call(
        ways_kernel,
        (meta, cots),
        [sds((256, 128), BF), sds((64, 256), BF), sds((64, 128), F32)],
        cost=small,
    )
    returning = call(return_kernel, (back, *ring), sds((256, FEAT), BF))
    returned = lax.all_to_all(returning.reshape(N_DP, 16, FEAT), "dp", 0, 0, tiled=True)
    grad_hidden = call(slots_kernel, (slot, weight, returned.reshape(256, FEAT)), sds((64, FEAT), BF))
    return logprobs.reshape(32), grad_hidden


def solution(mesh):
    return jax.shard_map(
        per_device,
        mesh=mesh,
        in_specs=(P("dp", "vocab"), P(None, ("dp", "vocab")), P(), P("dp"), P("dp"), P("dp")),
        out_specs=(P("dp"), P("dp", "vocab")),
        check_vma=False,
    )
```
